128 devices in a mesh: celly: 16 (over x, y), cellx: 8 (over z, core).
Axes of the slice: x: 4, y: 4, z: 4, core: 2. Of those that a mesh axis runs over, the one named last changes fastest.
Arguments:
- flux_blocks: bfloat16 [16384, 128, 128], P(('celly', 'cellx')), may hold values from -6 to 6
- ivar_blocks: bfloat16 [16384, 128, 128], P(('celly', 'cellx')), may hold values from 0.25 to 4
- dest_cell: int32 [16384, 1], P(('celly', 'cellx')), may hold values from 0 to 127; in each aligned block of 128 rows (0 to 127, 128 to 255, ...) at most 2 rows name the same one
- visit_id: int32 [16384], P(('celly', 'cellx')), may hold values from 0 to 19
- slot_id: int32 [16384], P(('celly', 'cellx')), may hold values from 0 to 3
- row_taps: bfloat16 [7, 41], replicated, may hold values from -1 to 1
- col_taps: bfloat16 [7, 41], replicated, may hold values from -1 to 1
- kernel_coef: float32 [20, 7, 3], replicated, may hold values from -3 to 3
Outputs:
- coadd: float32 [4096, 2048], P('celly', 'cellx')
- coadd_weight: float32 [4096, 2048], P('celly', 'cellx')
The draws below stay inside these ranges and needn't reach their ends.
Inputs may be any that keep to these rules, and one draw needn't show every extreme that they name: `dest_cell`: no more than 2 of the 128 blocks of one device name the same cell, a bound that some block reaches.
All inputs are finite; a program needn't handle non-finite values.
Results may differ from the reference program's by a relative error of at most 0.0048.
Values may be sent and summed in bfloat16 or wider, within the bound.
A program may use at most 128 MiB of HBM per device.

```python
import math
import jax
import jax.numpy as jnp
import numpy as np
from jax import lax

CELL = 256
BLOCK = 128
KTAPS = 41
HALF = 20
NBASIS = 7
VISITS = 20
BLK_DEV = 128
CAP = 2
TOTAL_BLK = 16384
ROWS_PIX = 4096
COLS_PIX = 2048
N_CELLY = 16
N_CELLX = 8
DEVICES = 128


def plant(values, stream_key, least, top_value):
    longest = values.shape.index(max(values.shape))
    spots = []
    for shift in (0, 1):
        where = [jax.random.randint(jax.random.fold_in(stream_key, axis), (), 0, length) for axis, length in enumerate(values.shape)]
        where[longest] = (where[longest] + shift) % values.shape[longest]
        spots.append(tuple(where))
    return values.at[spots[0]].set(least).at[spots[1]].set(top_value)


def steps_of(own_key, dims, split, least, top_value):
    level = 1.0
    for position, blocks in split:
        heights = jax.random.uniform(jax.random.fold_in(jax.random.fold_in(own_key, 6), position), (blocks,), jnp.float32, least / len(split), top_value / len(split))
        level = level * jnp.repeat(jnp.exp(heights), dims[position] // blocks).reshape((-1,) + (1,) * (len(dims) - 1 - position))
    return level


def deal_out(stream_key, own, number, rows, count, top, reach, skew):
    ranking = jax.random.permutation(stream_key, count)
    heavy_load, common = shares(count, rows * top, reach, skew, True), shares(count, rows * top, reach, skew, False)
    places = jnp.arange(count)

    def named(tallies, rotation):
        used = int((tallies > 0).sum())
        fixed = max(1, used // 4)
        shifted = fixed + (places - fixed + rotation * (used - fixed)) % max(1, count - fixed)
        return jnp.zeros((count,), jnp.int32).at[ranking[jnp.where(places < fixed, places, shifted)]].set(jnp.asarray(tallies, jnp.int32))

    tallies = jnp.where(number % 4 == 0, named(heavy_load, number // 4), named(common, number - number // 4 - 1))
    mixed = jax.random.permutation(jax.random.fold_in(own, 3), count)
    giver, taker = mixed[0:count // 2 * 2:2], mixed[1:count // 2 * 2:2]
    slack = jnp.minimum(tallies[giver] - 1, reach - tallies[taker]) // 2
    slack = jnp.where((giver == ranking[0]) | (taker == ranking[0]) | (tallies[taker] == 0), 0, jnp.maximum(slack, 0))
    shifted = jax.random.randint(jax.random.fold_in(own, 4), (count // 2,), 0, 1 << 20) % (slack + 1)
    tallies = tallies.at[giver].add(-shifted).at[taker].add(shifted)
    members = jnp.searchsorted(jnp.cumsum(tallies), jnp.arange(rows * top), side="right").astype(jnp.int32)
    listing = members.reshape(top, rows).T
    listing = listing[jax.random.permutation(jax.random.fold_in(own, 1), rows)]
    rotation = jax.random.randint(jax.random.fold_in(own, 2), (rows, 1), 0, top)
    return jnp.take_along_axis(listing, (jnp.arange(top)[None, :] + rotation) % top, axis=1)


def shares(number_of, total, most, skew, full):
    portions = [(1 << 20) // math.isqrt(standing ** skew) + 1 for standing in range(1, number_of + 1)]
    largest = most if full else min(most, max(-(-total // number_of), total * portions[0] // sum(portions)))
    least = 1 if total - largest >= number_of - 1 else 0
    holding, rest = [largest] + [least] * (number_of - 1), total - largest - least * (number_of - 1)
    while rest > 0:
        movable = [i for i in range(1, number_of) if holding[i] < largest] or [i for i in range(1, number_of) if holding[i] < most]
        mass, left = sum([portions[i] for i in movable]), rest
        for i in movable:
            extra = min(most - holding[i], max(1, left * portions[i] // mass), rest)
            holding[i] = holding[i] + extra
            rest = rest - extra
    return np.array(holding)


def normal_values(key, extent, scale, limit, shards=(), held_as=jnp.bfloat16):
    array = scale * jax.random.normal(key, extent, jnp.float32)
    if shards:
        array = array * steps_of(key, extent, shards, -0.22, 0.18)
    return jnp.clip(array, -limit, limit).astype(held_as)


def setup_inputs(seed: int = 0) -> dict:
    keys = jax.random.split(jax.random.key(seed), 9)
    flux_blocks = normal_values(keys[0], (TOTAL_BLK, BLOCK, BLOCK), 1.0, 6.0, ((0, 128),))
    ivar_blocks = jnp.clip(jnp.exp(math.log(4.0) - 2.7725887 * jax.random.uniform(keys[1], (TOTAL_BLK, BLOCK, BLOCK), jnp.float32) ** steps_of(keys[1], (TOTAL_BLK, BLOCK, BLOCK), ((0, 128),), -0.2, 0.2)), 0.25, 4.0).astype(jnp.bfloat16)
    dest_cell_keys = jax.random.split(jax.random.fold_in(keys[2], 1), TOTAL_BLK // BLK_DEV)
    dest_cell_turns = jax.random.permutation(jax.random.fold_in(keys[2], 3), TOTAL_BLK // BLK_DEV)
    dest_cell = jax.vmap(lambda own, number: deal_out(jax.random.fold_in(keys[2], 2), own, number, BLK_DEV, DEVICES, 1, CAP, 2))(dest_cell_keys, dest_cell_turns).reshape((TOTAL_BLK, 1))
    visit_id = plant(jax.random.randint(keys[3], (TOTAL_BLK,), 0, VISITS), jax.random.fold_in(keys[3], 1), 0, VISITS - 1).astype(jnp.int32)
    slot_id = plant(jax.random.randint(keys[4], (TOTAL_BLK,), 0, 4), jax.random.fold_in(keys[4], 1), 0, 3).astype(jnp.int32)
    row_taps = normal_values(keys[5], (NBASIS, KTAPS), KTAPS ** -0.5, 1.0)
    col_taps = normal_values(keys[6], (NBASIS, KTAPS), KTAPS ** -0.5, 1.0)
    kernel_coef = normal_values(keys[7], (VISITS, NBASIS, 3), 0.5, 3.0, (), jnp.float32)
    return dict(flux_blocks=flux_blocks, ivar_blocks=ivar_blocks, dest_cell=dest_cell, visit_id=visit_id, slot_id=slot_id, row_taps=row_taps, col_taps=col_taps, kernel_coef=kernel_coef)


def toeplitz_tables(taps, count, span):
    rows_index = jnp.arange(count)[:, None, None]
    cols_index = jnp.arange(span)[None, :, None]
    taps_index = jnp.arange(taps.shape[1])[None, None, :]
    picker = (cols_index - rows_index == taps_index).astype(jnp.float32)
    return jnp.einsum("ijp,bp->bij", picker, taps.astype(jnp.float32)).astype(jnp.bfloat16)


def build_plane(values, cell_row, cell_col, slot_row, slot_col, visit_id):
    shape = (VISITS, N_CELLY, N_CELLX, 2, 2, BLOCK, BLOCK)
    grid = jnp.zeros(shape, jnp.float32).at[visit_id, cell_row, cell_col, slot_row, slot_col].add(values.astype(jnp.float32))
    grid = grid.astype(jnp.bfloat16)
    grid = jnp.transpose(grid, (0, 1, 3, 5, 2, 4, 6))
    return grid.reshape(VISITS, ROWS_PIX, COLS_PIX)


def reference(flux_blocks, ivar_blocks, dest_cell, visit_id, slot_id, row_taps, col_taps, kernel_coef):
    target = dest_cell[:, 0]
    cell_row = target // N_CELLX
    cell_col = target % N_CELLX
    slot_row = slot_id // 2
    slot_col = slot_id % 2
    flux_plane = build_plane(flux_blocks, cell_row, cell_col, slot_row, slot_col, visit_id)
    ivar_plane = build_plane(ivar_blocks, cell_row, cell_col, slot_row, slot_col, visit_id)
    flux_padded = jnp.pad(flux_plane, ((0, 0), (HALF, HALF), (HALF, HALF)))
    span = CELL + 2 * HALF
    row_table = toeplitz_tables(row_taps, CELL, span).astype(jnp.float32)
    col_table = toeplitz_tables(col_taps, CELL, span).astype(jnp.float32)
    zero = jnp.zeros((), jnp.int32)

    def one_cell(index):
        top = (index // N_CELLX) * CELL
        left = (index % N_CELLX) * CELL
        window = lax.dynamic_slice(flux_padded, (zero, top, left), (VISITS, span, span)).astype(jnp.float32)
        weights = lax.dynamic_slice(ivar_plane, (zero, top, left), (VISITS, CELL, CELL)).astype(jnp.float32)
        first = jnp.einsum("bip,vpq->vbiq", row_table, window).astype(jnp.bfloat16)
        second = jnp.einsum("vbiq,bkq->vbik", first.astype(jnp.float32), col_table)
        rows_pos = ((top + jnp.arange(CELL)).astype(jnp.float32) + 0.5) * (2.0 / ROWS_PIX) - 1.0
        cols_pos = ((left + jnp.arange(CELL)).astype(jnp.float32) + 0.5) * (2.0 / COLS_PIX) - 1.0
        coef = kernel_coef.astype(jnp.float32)
        basis_weight = coef[:, :, 0, None, None] + coef[:, :, 1, None, None] * rows_pos[None, None, :, None] + coef[:, :, 2, None, None] * cols_pos[None, None, None, :]
        matched = jnp.sum(basis_weight * second, axis=1)
        numer = jnp.sum(weights * matched, axis=0)
        total = 1.0 + jnp.sum(weights, axis=0)
        return numer / total, total

    coadd_cells, weight_cells = lax.map(one_cell, jnp.arange(N_CELLY * N_CELLX, dtype=jnp.int32))

    def arrange(cells):
        cells = cells.reshape(N_CELLY, N_CELLX, CELL, CELL)
        return jnp.transpose(cells, (0, 2, 1, 3)).reshape(ROWS_PIX, COLS_PIX)

    return arrange(coadd_cells), arrange(weight_cells)
```

```python
import functools

import jax
import jax.numpy as jnp
from jax import lax
from jax.experimental import pallas as pl
from jax.experimental.pallas import tpu as pltpu
from jax.sharding import PartitionSpec as P

MESH = pl.DeviceIdType.MESH
SIDE = 4
CHIPS = SIDE**3
EDGE = 32
GROUP = 4


def toeplitz_tables(taps, count, offsets):
    half = (taps.shape[1] - 1) // 2
    index = offsets[None, :] + half - jnp.arange(count)[:, None]
    picker = (index[:, :, None] == jnp.arange(taps.shape[1])).astype(jnp.float32)
    return jnp.einsum("ijp,bp->bij", picker, taps.astype(jnp.float32)).astype(jnp.bfloat16)


def coordinates():
    row, col = lax.axis_index("celly"), lax.axis_index("cellx")
    return [row // SIDE, row % SIDE, col // 2, col % 2]


def device(q):
    return (q[0] * SIDE + q[1], q[2] * 2 + q[3])


def shifted(q, axis, d, n=SIDE):
    r = list(q)
    r[axis] = lax.rem(q[axis] + d, n)
    return r


def gather_kernel(index_ref, flux_ref, ivar_ref, out_ref):
    arr = pl.program_id(0)
    step = pl.program_id(1)
    per = out_ref.shape[0]

    def pick(ref):
        def body(i, carry):
            out_ref[i] = ref[index_ref[step * per + i]]
            return carry

        lax.fori_loop(0, per, body, 0)

    pl.when(arr == 0)(lambda: pick(flux_ref))
    pl.when(arr == 1)(lambda: pick(ivar_ref))


def units_of(slots):
    units = [(s, 0, 128, s) for s in range(3)]
    if slots == 4:
        units += [(3, 0, 48, 0), (3, 48, 48, 1), (3, 96, 32, 2)]
    return units


def route_kernel(
    slots, visits, bases,
    order_ref, fresh_ref, last_ref, has_ref, coef_ref, t0, rowt_ref, colt_ref,
    numer_out, total_out, t1, t2,
    t_flux, t_ivar, seg, win, matched, strips, got,
    s1, r1, s2, r2, s3, r3, s4, r4, ls, hs, hr,
):
    t = (t_flux, t_ivar)
    q = coordinates()
    row, col = lax.axis_index("celly"), lax.axis_index("cellx")
    rows_n, cols_n = lax.axis_size("celly"), lax.axis_size("cellx")
    units = units_of(slots)
    count = len(units)
    partner = shifted(q, 3, 1, 2)
    above = (lax.rem(row + rows_n - 1, rows_n), col)
    below = (lax.rem(row + 1, rows_n), col)
    left = (row, lax.rem(col + cols_n - 1, cols_n))
    right = (row, lax.rem(col + 1, cols_n))

    barrier = pltpu.get_barrier_semaphore()
    peers = [device(shifted(q, a, d)) for a in range(3) for d in (1, 2, 3)]
    peers += [device(partner), above, below, left, right]
    for peer in peers:
        pl.semaphore_signal(barrier, inc=1, device_id=peer, device_id_type=MESH)
    pl.semaphore_wait(barrier, len(peers))

    def remote(src, dst, send, recv, to):
        return pltpu.make_async_remote_copy(
            src, dst, send, recv, device_id=to, device_id_type=MESH
        )

    def at(ref, unit, lead, where):
        slot, start, rows, _ = units[unit]
        index = [where.get(axis, slice(None)) for axis in range(3)]
        return ref.at[(*lead, slot, *index, pl.ds(start, rows))]

    def axes(unit):
        a = units[unit][3]
        return a, (a + 1) % 3, (a + 2) % 3

    def first_hop(arr, u, d):
        a, b, c = axes(u)
        to = shifted(q, a, d)
        return remote(
            at(t0, u, (arr,), {a: to[a]}), at(t1, u, (arr,), {a: q[a]}),
            s1.at[arr, u, d], r1.at[arr, u, q[a]], device(to),
        )

    def first_arrival(arr, u, da):
        a, b, c = axes(u)
        asrc = lax.rem(q[a] + da, SIDE)
        place = at(t1, u, (arr,), {a: asrc})
        return remote(place, place, s1.at[arr, u, da], r1.at[arr, u, asrc], device(q))

    def second_hop(arr, u, da, d):
        a, b, c = axes(u)
        to = shifted(q, b, d)
        asrc = lax.rem(q[a] + da, SIDE)
        return remote(
            at(t0 if da == 0 else t1, u, (arr,), {a: asrc, b: to[b]}),
            at(t2, u, (arr,), {a: asrc, b: q[b]}),
            s2.at[arr, u, d, da], r2.at[arr, u, q[b], asrc], device(to),
        )

    def second_arrival(arr, u, db, da):
        a, b, c = axes(u)
        asrc = lax.rem(q[a] + da, SIDE)
        bsrc = lax.rem(q[b] + db, SIDE)
        place = at(t2, u, (arr,), {a: asrc, b: bsrc})
        return remote(place, place, s2.at[arr, u, db, da], r2.at[arr, u, bsrc, asrc], device(q))

    def third_sources(arr, u, db, cc):
        a, b, c = axes(u)
        bsrc = lax.rem(q[b] + db, SIDE)
        if db:
            return [(at(t2, u, (arr,), {b: bsrc, c: cc}), {b: bsrc, c: q[c]})]
        pairs = []
        for da in range(SIDE):
            asrc = lax.rem(q[a] + da, SIDE)
            source = at(t0 if da == 0 else t1, u, (arr,), {a: asrc, b: bsrc, c: cc})
            pairs.append((source, {a: asrc, b: bsrc, c: q[c]}))
        return pairs

    def third_hop(arr, u, db, d):
        a, b, c = axes(u)
        to = shifted(q, c, d)
        bsrc = lax.rem(q[b] + db, SIDE)
        return [
            remote(source, at(t[arr], u, (0,), where), s3.at[arr, u, d, db], r3.at[arr, u, q[c], bsrc], device(to))
            for source, where in third_sources(arr, u, db, to[c])
        ]

    def third_whole(arr, u, db, d):
        a, b, c = axes(u)
        bsrc = lax.rem(q[b] + db, SIDE)
        csrc = lax.rem(q[c] + d, SIDE)
        place = at(t[arr], u, (0,), {b: bsrc, c: csrc})
        return remote(place, place, s3.at[arr, u, d, db], r3.at[arr, u, csrc, bsrc], device(q))

    def third_stay(arr, u, db):
        a, b, c = axes(u)
        return [
            pltpu.make_async_copy(source, at(t[arr], u, (0,), where), ls.at[arr, u, db])
            for source, where in third_sources(arr, u, db, q[c])
        ]

    def stay_whole(arr, u, db):
        a, b, c = axes(u)
        place = at(t[arr], u, (0,), {b: lax.rem(q[b] + db, SIDE), c: q[c]})
        return pltpu.make_async_copy(place, place, ls.at[arr, u, db])

    def fourth_hop(arr, u, dc):
        a, b, c = axes(u)
        csrc = lax.rem(q[c] + dc, SIDE)
        return remote(
            at(t[arr], u, (0,), {c: csrc}), at(t[arr], u, (1,), {c: csrc}),
            s4.at[arr, u, dc], r4.at[arr, u, csrc], device(partner),
        )

    def stage1(arr):
        for d in (2, 1, 3):
            for u in range(count):
                first_hop(arr, u, d).start()

    def stage2(arr):
        for da in (0, 1, 3, 2):
            for u in range(count):
                if da:
                    first_arrival(arr, u, da).wait_recv()
                for d in (2, 1, 3):
                    second_hop(arr, u, da, d).start()

    def stage3(arr):
        for db in (0, 1, 3, 2):
            for u in range(count):
                if db:
                    for da in range(SIDE):
                        second_arrival(arr, u, db, da).wait_recv()
                for d in (2, 1, 3):
                    for copy in third_hop(arr, u, db, d):
                        copy.start()
                for copy in third_stay(arr, u, db):
                    copy.start()

    def stage4(arr):
        for dc in (0, 1, 3, 2):
            for u in range(count):
                for db in range(SIDE):
                    if dc:
                        third_whole(arr, u, db, dc).wait_recv()
                    else:
                        stay_whole(arr, u, db).wait()
                fourth_hop(arr, u, dc).start()
        for dc in (0, 1, 3, 2):
            for u in range(count):
                fourth_hop(arr, u, dc).wait()

    def drain(arr):
        for u in range(count):
            for d in (1, 2, 3):
                first_hop(arr, u, d).wait_send()
                for e in range(SIDE):
                    second_hop(arr, u, e, d).wait_send()
                    third_whole(arr, u, e, d).wait_send()

    def segments(arr):
        def body(p, total):
            i = order_ref[p]
            block = t[arr][i // (CHIPS * slots), (i // CHIPS) % slots,
                      (i // 16) % 4, (i // 4) % 4, i % 4].astype(jnp.float32)
            total = jnp.where(fresh_ref[p] > 0, block, total + block)
            seg[p] = total.astype(jnp.bfloat16)
            return total

        lax.fori_loop(0, seg.shape[0], body, jnp.zeros((128, 128), jnp.float32))

    def summed(key):
        block = seg[last_ref[key]]
        return jnp.where(has_ref[key] > 0, block, jnp.zeros_like(block))

    def place_flux():
        def body(v, carry):
            for sr in range(2):
                for sc in range(2):
                    win[v, 128 * sr : 128 * sr + 128, 128 * sc : 128 * sc + 128] = summed(
                        v * 4 + sr * 2 + sc
                    )
            return carry

        lax.fori_loop(0, visits, body, 0)

    down = remote(
        win.at[:, pl.ds(256 - EDGE, EDGE), pl.ds(0, 256)],
        win.at[:, pl.ds(256, EDGE), pl.ds(0, 256)],
        hs.at[0], hr.at[0], below,
    )
    up = remote(
        win.at[:, pl.ds(0, EDGE), pl.ds(0, 256)],
        win.at[:, pl.ds(256 + EDGE, EDGE), pl.ds(0, 256)],
        hs.at[1], hr.at[1], above,
    )
    to_right = remote(strips.at[0], got.at[0], hs.at[2], hr.at[2], right)
    to_left = remote(strips.at[1], got.at[1], hs.at[3], hr.at[3], left)

    def pack_columns():
        top_ok = (row > 0).astype(jnp.float32)
        bottom_ok = (row < rows_n - 1).astype(jnp.float32)

        def clear(v, carry):
            lo = win[v, 256 : 256 + EDGE, 0:256].astype(jnp.float32) * top_ok
            hi = win[v, 256 + EDGE : 256 + 2 * EDGE, 0:256].astype(jnp.float32) * bottom_ok
            win[v, 256 : 256 + EDGE, 0:256] = lo.astype(jnp.bfloat16)
            win[v, 256 + EDGE : 256 + 2 * EDGE, 0:256] = hi.astype(jnp.bfloat16)
            return carry

        lax.fori_loop(0, visits, clear, 0)
        lane = lax.broadcasted_iota(jnp.int32, (256 + 2 * EDGE, 128), 1)

        def body(g, carry):
            ends = jnp.zeros(lane.shape, jnp.float32)
            starts = jnp.zeros(lane.shape, jnp.float32)
            for k in range(GROUP):
                mine = (lane >= EDGE * k) & (lane < EDGE * k + EDGE)
                tail = win[g * GROUP + k, :, 128:256].astype(jnp.float32)
                head = win[g * GROUP + k, :, 0:128].astype(jnp.float32)
                ends = jnp.where(mine, pltpu.roll(tail, (EDGE * k + EDGE) % 128, 1), ends)
                starts = jnp.where(mine, pltpu.roll(head, EDGE * k, 1) if k else head, starts)
            strips[0, g] = ends.astype(jnp.bfloat16)
            strips[1, g] = starts.astype(jnp.bfloat16)
            return carry

        lax.fori_loop(0, visits // GROUP, body, 0)

    def unpack_columns():
        left_ok = (col > 0).astype(jnp.float32)
        right_ok = (col < cols_n - 1).astype(jnp.float32)
        lane = lax.broadcasted_iota(jnp.int32, (256 + 2 * EDGE, 128), 1)

        def body(g, carry):
            lefts = got[0, g].astype(jnp.float32) * left_ok
            rights = got[1, g].astype(jnp.float32) * right_ok
            for k in range(GROUP):
                lo = pltpu.roll(lefts, (128 - EDGE * k) % 128, 1) if k else lefts
                hi = pltpu.roll(rights, (128 + EDGE - EDGE * k) % 128, 1) if k != 1 else rights
                tile = jnp.where(lane < EDGE, lo, jnp.where(lane < 2 * EDGE, hi, 0.0))
                win[g * GROUP + k, :, 256:384] = tile.astype(jnp.bfloat16)
            return carry

        lax.fori_loop(0, visits // GROUP, body, 0)

    def position(index, axis, size):
        pixel = (index * 256 + lax.broadcasted_iota(jnp.int32, (256, 256), axis)).astype(jnp.float32)
        return (pixel + 0.5) * (2.0 / (256 * size)) - 1.0

    def correlate(start, stop):
        def body(v, carry):
            rows_pos = position(row, 0, rows_n)
            cols_pos = position(col, 1, cols_n)
            window = win[v]
            acc = jnp.zeros((256, 256), jnp.float32)
            for b in range(bases):
                first = jnp.dot(rowt_ref[b], window, preferred_element_type=jnp.float32)
                second = jnp.dot(
                    first.astype(jnp.bfloat16), colt_ref[b], preferred_element_type=jnp.float32
                )
                weight = coef_ref[v, b * 3] + coef_ref[v, b * 3 + 1] * rows_pos
                acc += (weight + coef_ref[v, b * 3 + 2] * cols_pos) * second
            matched[v] = acc
            return carry

        lax.fori_loop(start, stop, body, 0)

    def combine():
        for sr in range(2):
            for sc in range(2):
                rows, cols = slice(128 * sr, 128 * sr + 128), slice(128 * sc, 128 * sc + 128)

                def body(v, carry, rows=rows, cols=cols, quarter=sr * 2 + sc):
                    numer, total = carry
                    weight = summed(v * 4 + quarter).astype(jnp.float32)
                    return numer + weight * matched[v, rows, cols], total + weight

                zero = jnp.zeros((128, 128), jnp.float32)
                numer, total = lax.fori_loop(0, visits, body, (zero, zero + 1.0))
                numer_out[rows, cols] = numer / total
                total_out[rows, cols] = total

    stage1(0)
    stage2(0)
    stage3(0)
    stage1(1)
    stage4(0)
    segments(0)
    place_flux()
    down.start()
    up.start()
    stage2(1)
    down.wait()
    up.wait()
    pack_columns()
    to_right.start()
    to_left.start()
    to_right.wait()
    to_left.wait()
    unpack_columns()
    correlate(0, visits // 2)
    stage3(1)
    correlate(visits // 2, visits)
    stage4(1)
    segments(1)
    combine()
    drain(0)
    drain(1)


def route(slots, collective, order, fresh, last, has, coef, send, row_table, col_table):
    visits, bases = coef.shape[0], row_table.shape[0]
    count = len(units_of(slots))
    dma = pltpu.SemaphoreType.DMA
    hop = jax.ShapeDtypeStruct((2, slots, 4, 4, 4, 128, 128), jnp.bfloat16)
    image = jax.ShapeDtypeStruct((256, 256), jnp.float32)
    smem = pl.BlockSpec(memory_space=pltpu.SMEM)
    vmem = pl.BlockSpec(memory_space=pltpu.VMEM)
    anywhere = pl.BlockSpec(memory_space=pl.ANY)
    coadd, weight, _, _ = pl.pallas_call(
        functools.partial(route_kernel, slots, visits, bases),
        out_shape=[image, image, hop, hop],
        in_specs=[smem] * 5 + [anywhere] + [vmem] * 2,
        out_specs=[vmem] * 2 + [anywhere] * 2,
        scratch_shapes=[
            pltpu.VMEM((2, slots, 4, 4, 4, 128, 128), jnp.bfloat16),
            pltpu.VMEM((2, slots, 4, 4, 4, 128, 128), jnp.bfloat16),
            pltpu.VMEM((256, 128, 128), jnp.bfloat16),
            pltpu.VMEM((visits, 256 + 2 * EDGE, 384), jnp.bfloat16),
            pltpu.VMEM((visits, 256, 256), jnp.float32),
            pltpu.VMEM((2, visits // GROUP, 256 + 2 * EDGE, 128), jnp.bfloat16),
            pltpu.VMEM((2, visits // GROUP, 256 + 2 * EDGE, 128), jnp.bfloat16),
            dma((2, count, 4)), dma((2, count, 4)),
            dma((2, count, 4, 4)), dma((2, count, 4, 4)),
            dma((2, count, 4, 4)), dma((2, count, 4, 4)),
            dma((2, count, 4)), dma((2, count, 4)),
            dma((2, count, 4)), dma((4,)), dma((4,)),
        ],
        compiler_params=pltpu.CompilerParams(
            collective_id=collective, has_side_effects=True, vmem_limit_bytes=63 * 2**20
        ),
    )(order, fresh, last, has, coef, send, row_table, col_table)
    return coadd, weight


def local(flux_blocks, ivar_blocks, dest_cell, visit_id, slot_id, row_taps, col_taps, kernel_coef):
    slots = 4
    blocks = flux_blocks.shape[0]
    visits, bases = kernel_coef.shape[:2]
    bins = visits * 4
    me_row, me_col = lax.axis_index("celly"), lax.axis_index("cellx")
    my_chip, my_core = me_row * 4 + me_col // 2, me_col % 2

    target = dest_cell[:, 0]
    chip = target // 2
    i = jnp.arange(blocks)
    rank = jnp.sum((chip[:, None] == chip[None, :]) & (i[None, :] < i[:, None]), axis=1)
    spot = rank * CHIPS + chip
    hit = spot[None, :] == jnp.arange(slots * CHIPS)[:, None]
    index = jnp.sum(jnp.where(hit, i[None, :], 0), axis=1).astype(jnp.int32)
    code = (target % 2) * bins + visit_id * 4 + slot_id
    tags = jnp.sum(jnp.where(hit, code[None, :] + 1, 0), axis=1) - 1
    tags = lax.all_gather(tags.astype(jnp.int32), ("celly", "cellx"), axis=0, tiled=False)

    def gathered(number):
        per = 32
        return pl.pallas_call(
            gather_kernel,
            out_shape=jax.ShapeDtypeStruct((2, number, CHIPS, 128, 128), jnp.bfloat16),
            grid_spec=pltpu.PrefetchScalarGridSpec(
                num_scalar_prefetch=1,
                grid=(2, number * CHIPS // per),
                in_specs=[pl.BlockSpec((blocks, 128, 128), lambda a, s, ix: (0, 0, 0))] * 2,
                out_specs=pl.BlockSpec(
                    (None, None, per, 128, 128),
                    lambda a, s, ix: (a, s // (CHIPS // per), s % (CHIPS // per), 0, 0),
                ),
            ),
            compiler_params=pltpu.CompilerParams(vmem_limit_bytes=40 * 2**20),
        )(index, flux_blocks, ivar_blocks).reshape(2, number, 4, 4, 4, 128, 128)

    mine = lax.dynamic_index_in_dim(
        tags.reshape(CHIPS, 2, slots, CHIPS), my_chip, axis=3, keepdims=False
    )
    lanes = jnp.where(my_core == 0, mine, mine[:, ::-1])
    overflow = jnp.any(tags[:, 3 * CHIPS :] >= 0)

    window = jnp.arange(256)
    edge = jnp.arange(EDGE)
    far = jnp.full((128 - 2 * EDGE,), -1000)
    offsets = jnp.concatenate([window, edge - EDGE, edge + 256])
    row_table = toeplitz_tables(row_taps, 256, offsets)
    col_table = toeplitz_tables(col_taps, 256, jnp.concatenate([offsets, far])).transpose(0, 2, 1)
    coef = kernel_coef.reshape(visits, bases * 3)

    def run(number, collective):
        keys = jnp.transpose(lanes[:, :, :number], (1, 2, 0)).reshape(-1) - my_core * bins
        total = keys.shape[0]
        keys = jnp.where((keys >= 0) & (keys < bins), keys, bins)
        order_key = keys * total + jnp.arange(total)
        rank_of = jnp.sum((order_key[None, :] < order_key[:, None]).astype(jnp.int32), axis=1)
        spots = jnp.arange(256)
        order = jnp.sum(
            jnp.where(rank_of[None, :] == spots[:, None], jnp.arange(total)[None, :], 0), axis=1
        ).astype(jnp.int32)
        bin_ids = jnp.arange(bins)
        upto = jnp.sum((keys[None, :] <= bin_ids[:, None]).astype(jnp.int32), axis=1)
        below = jnp.sum((keys[None, :] < bin_ids[:, None]).astype(jnp.int32), axis=1)
        has = (upto > below).astype(jnp.int32)
        fresh = jnp.any(
            (below[None, :] == spots[:, None]) & (has[None, :] > 0), axis=1
        ).astype(jnp.int32)
        last = jnp.maximum(upto - 1, 0).astype(jnp.int32)
        return route(
            number, collective, order, fresh, last, has, coef, gathered(number),
            row_table, col_table,
        )

    return lax.cond(overflow, lambda: run(4, 1), lambda: run(3, 0))


def solution(mesh):
    placed = (
        P(("celly", "cellx"), None, None),
        P(("celly", "cellx"), None, None),
        P(("celly", "cellx"), None),
        P(("celly", "cellx")),
        P(("celly", "cellx")),
        P(),
        P(),
        P(),
    )
    return jax.shard_map(
        local,
        mesh=mesh,
        in_specs=placed,
        out_specs=(P("celly", "cellx"), P("celly", "cellx")),
        check_vma=False,
    )
```

```python
import functools

import jax
import jax.numpy as jnp
from jax import lax
from jax.experimental import pallas as pl
from jax.experimental.pallas import tpu as pltpu
from jax.sharding import PartitionSpec as P

MESH = pl.DeviceIdType.MESH
SIDE = 4
CHIPS = SIDE**3
EDGE = 32
GROUP = 4


def coordinates():
    row, col = lax.axis_index("celly"), lax.axis_index("cellx")
    return [row // SIDE, row % SIDE, col // 2, col % 2]


def device(q):
    return (q[0] * SIDE + q[1], q[2] * 2 + q[3])


def shifted(q, axis, d, n=SIDE):
    r = list(q)
    r[axis] = lax.rem(q[axis] + d, n)
    return r


def gather_kernel(index_ref, flux_ref, ivar_ref, tag_ref, out_ref, all_ref, send, recv, own):
    arr, step = pl.program_id(0), pl.program_id(1)
    per = out_ref.shape[0]
    now = arr * pl.num_programs(1) + step
    x, y, z, core = q = coordinates()
    partner = shifted(q, 3, 1, 2)
    whole = slice(None)
    hops = [
        [(0, partner, (x, y, z, core))],
        [(d, shifted(q, 0, d), (x, y, z)) for d in (1, 2, 3)],
        [(d, shifted(q, 1, d), (whole, y, z)) for d in (1, 2, 3)],
        [(d, shifted(q, 2, d), (whole, whole, z)) for d in (1, 2, 3)],
    ]
    arrivals = [
        [(0, (x, y, z, 1 - core))],
        [(d, (lax.rem(x + SIDE - d, SIDE), y, z)) for d in (1, 2, 3)],
        [(d, (whole, lax.rem(y + SIDE - d, SIDE), z)) for d in (1, 2, 3)],
        [(d, (whole, whole, lax.rem(z + SIDE - d, SIDE))) for d in (1, 2, 3)],
    ]

    def copies(hop):
        return [
            pltpu.make_async_remote_copy(
                tag_ref if hop == 0 else all_ref.at[where], all_ref.at[where],
                send.at[hop, d], recv.at[hop, d], device_id=device(to), device_id_type=MESH,
            )
            for d, to, where in hops[hop]
        ]

    def begin():
        barrier = pltpu.get_barrier_semaphore()
        peers = [device(shifted(q, a, d)) for a in range(3) for d in (1, 2, 3)] + [device(partner)]
        for peer in peers:
            pl.semaphore_signal(barrier, inc=1, device_id=peer, device_id_type=MESH)
        mine = pltpu.make_async_copy(tag_ref, all_ref.at[x, y, z, core], own)
        mine.start()
        pl.semaphore_wait(barrier, len(peers))
        for copy in copies(0):
            copy.start()
        mine.wait()

    def advance(hop):
        for d, where in arrivals[hop]:
            place = all_ref.at[where]
            pltpu.make_async_remote_copy(
                place, place, send.at[hop, d], recv.at[hop, d],
                device_id=device(partner), device_id_type=MESH,
            ).wait_recv()
        if hop < 3:
            for copy in copies(hop + 1):
                copy.start()
        else:
            for earlier in range(4):
                for copy in copies(earlier):
                    copy.wait_send()

    pl.when(now == 0)(begin)

    def pick(ref):
        def body(i, carry):
            for k in range(4):
                out_ref[4 * i + k] = ref[index_ref[step * per + 4 * i + k]]
            return carry

        lax.fori_loop(0, per // 4, body, 0)

    pl.when(arr == 0)(lambda: pick(flux_ref))
    pl.when(arr == 1)(lambda: pick(ivar_ref))
    for hop, moment in enumerate((2, 6, 10, 15)):
        pl.when(now == moment)(functools.partial(advance, hop))


def units_of(slots):
    units = [(s, 0, 128, s) for s in range(3)]
    if slots == 4:
        units += [(3, 0, 48, 0), (3, 48, 48, 1), (3, 96, 32, 2)]
    return units


def route_kernel(
    slots, visits, bases,
    order_ref, fresh_ref, last_ref, has_ref, coef_ref, rtaps_ref, ctaps_ref, t0,
    numer_out, total_out, t1, t2,
    t_flux, t_ivar, seg, win, matched, strips, got, row_table, col_table, first_ref,
    s1, r1, s2, r2, s3, r3, s4, r4, ls, hs, hr,
):
    t = (t_flux, t_ivar)
    q = coordinates()
    row, col = lax.axis_index("celly"), lax.axis_index("cellx")
    rows_n, cols_n = lax.axis_size("celly"), lax.axis_size("cellx")
    taps = rtaps_ref.shape[1]
    half = (taps - 1) // 2
    units = units_of(slots)
    count = len(units)
    partner = shifted(q, 3, 1, 2)
    above = (lax.rem(row + rows_n - 1, rows_n), col)
    below = (lax.rem(row + 1, rows_n), col)
    left = (row, lax.rem(col + cols_n - 1, cols_n))
    right = (row, lax.rem(col + 1, cols_n))

    barrier = pltpu.get_barrier_semaphore()
    peers = [device(shifted(q, a, d)) for a in range(3) for d in (1, 2, 3)]
    peers += [device(partner), above, below, left, right]
    for peer in peers:
        pl.semaphore_signal(barrier, inc=1, device_id=peer, device_id_type=MESH)
    pl.semaphore_wait(barrier, len(peers))

    def remote(src, dst, send, recv, to):
        return pltpu.make_async_remote_copy(
            src, dst, send, recv, device_id=to, device_id_type=MESH
        )

    def at(ref, unit, lead, where):
        slot, start, rows, _ = units[unit]
        index = [where.get(axis, slice(None)) for axis in range(3)]
        return ref.at[(*lead, slot, *index, pl.ds(start, rows))]

    def axes(unit):
        a = units[unit][3]
        return a, (a + 1) % 3, (a + 2) % 3

    def first_hop(arr, u, d):
        a, b, c = axes(u)
        to = shifted(q, a, d)
        return remote(
            at(t0, u, (arr,), {a: to[a]}), at(t1, u, (arr,), {a: q[a]}),
            s1.at[arr, u, d], r1.at[arr, u, q[a]], device(to),
        )

    def first_arrival(arr, u, da):
        a, b, c = axes(u)
        asrc = lax.rem(q[a] + da, SIDE)
        place = at(t1, u, (arr,), {a: asrc})
        return remote(place, place, s1.at[arr, u, da], r1.at[arr, u, asrc], device(q))

    def second_hop(arr, u, da, d):
        a, b, c = axes(u)
        to = shifted(q, b, d)
        asrc = lax.rem(q[a] + da, SIDE)
        return remote(
            at(t0 if da == 0 else t1, u, (arr,), {a: asrc, b: to[b]}),
            at(t2, u, (arr,), {a: asrc, b: q[b]}),
            s2.at[arr, u, d, da], r2.at[arr, u, q[b], asrc], device(to),
        )

    def second_arrival(arr, u, db, da):
        a, b, c = axes(u)
        asrc = lax.rem(q[a] + da, SIDE)
        bsrc = lax.rem(q[b] + db, SIDE)
        place = at(t2, u, (arr,), {a: asrc, b: bsrc})
        return remote(place, place, s2.at[arr, u, db, da], r2.at[arr, u, bsrc, asrc], device(q))

    def third_sources(arr, u, db, cc):
        a, b, c = axes(u)
        bsrc = lax.rem(q[b] + db, SIDE)
        if db:
            return [(at(t2, u, (arr,), {b: bsrc, c: cc}), {b: bsrc, c: q[c]})]
        pairs = []
        for da in range(SIDE):
            asrc = lax.rem(q[a] + da, SIDE)
            source = at(t0 if da == 0 else t1, u, (arr,), {a: asrc, b: bsrc, c: cc})
            pairs.append((source, {a: asrc, b: bsrc, c: q[c]}))
        return pairs

    def third_hop(arr, u, db, d):
        a, b, c = axes(u)
        to = shifted(q, c, d)
        bsrc = lax.rem(q[b] + db, SIDE)
        return [
            remote(source, at(t[arr], u, (0,), where), s3.at[arr, u, d, db], r3.at[arr, u, q[c], bsrc], device(to))
            for source, where in third_sources(arr, u, db, to[c])
        ]

    def third_whole(arr, u, db, d):
        a, b, c = axes(u)
        bsrc = lax.rem(q[b] + db, SIDE)
        csrc = lax.rem(q[c] + d, SIDE)
        place = at(t[arr], u, (0,), {b: bsrc, c: csrc})
        return remote(place, place, s3.at[arr, u, d, db], r3.at[arr, u, csrc, bsrc], device(q))

    def third_stay(arr, u, db):
        a, b, c = axes(u)
        return [
            pltpu.make_async_copy(source, at(t[arr], u, (0,), where), ls.at[arr, u, db])
            for source, where in third_sources(arr, u, db, q[c])
        ]

    def stay_whole(arr, u, db):
        a, b, c = axes(u)
        place = at(t[arr], u, (0,), {b: lax.rem(q[b] + db, SIDE), c: q[c]})
        return pltpu.make_async_copy(place, place, ls.at[arr, u, db])

    def fourth_hop(arr, u, dc):
        a, b, c = axes(u)
        csrc = lax.rem(q[c] + dc, SIDE)
        return remote(
            at(t[arr], u, (0,), {c: csrc}), at(t[arr], u, (1,), {c: csrc}),
            s4.at[arr, u, dc], r4.at[arr, u, csrc], device(partner),
        )

    def stage1(arr):
        for d in (2, 1, 3):
            for u in range(count):
                first_hop(arr, u, d).start()

    def stage2(arr):
        for da in (0, 1, 3, 2):
            for u in range(count):
                if da:
                    first_arrival(arr, u, da).wait_recv()
                for d in (2, 1, 3):
                    second_hop(arr, u, da, d).start()

    def stage3(arr, groups=(0, 1, 3, 2)):
        for db in groups:
            for u in range(count):
                if db:
                    for da in range(SIDE):
                        second_arrival(arr, u, db, da).wait_recv()
                for d in (2, 1, 3):
                    for copy in third_hop(arr, u, db, d):
                        copy.start()
                for copy in third_stay(arr, u, db):
                    copy.start()

    def stage4(arr):
        for dc in (0, 1, 3, 2):
            for u in range(count):
                for db in range(SIDE):
                    if dc:
                        third_whole(arr, u, db, dc).wait_recv()
                    else:
                        stay_whole(arr, u, db).wait()
                fourth_hop(arr, u, dc).start()
        for dc in (0, 1, 3, 2):
            for u in range(count):
                fourth_hop(arr, u, dc).wait()

    def drain(arr):
        for u in range(count):
            for d in (1, 2, 3):
                first_hop(arr, u, d).wait_send()
                for e in range(SIDE):
                    second_hop(arr, u, e, d).wait_send()
                    third_whole(arr, u, e, d).wait_send()

    def segments(arr):
        def body(p, total):
            i = order_ref[p]
            block = t[arr][i // (CHIPS * slots), (i // CHIPS) % slots,
                      (i // 16) % 4, (i // 4) % 4, i % 4].astype(jnp.float32)
            total = jnp.where(fresh_ref[p] > 0, block, total + block)
            seg[p] = total.astype(jnp.bfloat16)
            return total

        lax.fori_loop(0, seg.shape[0], body, jnp.zeros((128, 128), jnp.float32))

    def summed(key):
        block = seg[last_ref[key]]
        return jnp.where(has_ref[key] > 0, block, jnp.zeros_like(block))

    def place_flux():
        def body(v, carry):
            for sr in range(2):
                for sc in range(2):
                    win[v, EDGE + 128 * sr : EDGE + 128 * sr + 128, 128 * sc : 128 * sc + 128] = summed(
                        v * 4 + sr * 2 + sc
                    )
            return carry

        lax.fori_loop(0, visits, body, 0)

    down = remote(
        win.at[:, pl.ds(256, EDGE), pl.ds(0, 256)],
        win.at[:, pl.ds(0, EDGE), pl.ds(0, 256)],
        hs.at[0], hr.at[0], below,
    )
    up = remote(
        win.at[:, pl.ds(EDGE, EDGE), pl.ds(0, 256)],
        win.at[:, pl.ds(256 + EDGE, EDGE), pl.ds(0, 256)],
        hs.at[1], hr.at[1], above,
    )
    to_right = remote(strips.at[0], got.at[0], hs.at[2], hr.at[2], right)
    to_left = remote(strips.at[1], got.at[1], hs.at[3], hr.at[3], left)

    def pack_columns():
        top_ok = (row > 0).astype(jnp.float32)
        bottom_ok = (row < rows_n - 1).astype(jnp.float32)

        def clear(v, carry):
            lo = win[v, 0:EDGE, 0:256].astype(jnp.float32) * top_ok
            hi = win[v, 256 + EDGE : 256 + 2 * EDGE, 0:256].astype(jnp.float32) * bottom_ok
            win[v, 0:EDGE, 0:256] = lo.astype(jnp.bfloat16)
            win[v, 256 + EDGE : 256 + 2 * EDGE, 0:256] = hi.astype(jnp.bfloat16)
            return carry

        lax.fori_loop(0, visits, clear, 0)
        lane = lax.broadcasted_iota(jnp.int32, (256 + 2 * EDGE, 128), 1)

        def body(g, carry):
            ends = jnp.zeros(lane.shape, jnp.float32)
            starts = jnp.zeros(lane.shape, jnp.float32)
            for k in range(GROUP):
                mine = (lane >= EDGE * k) & (lane < EDGE * k + EDGE)
                tail = win[g * GROUP + k, :, 128:256].astype(jnp.float32)
                head = win[g * GROUP + k, :, 0:128].astype(jnp.float32)
                ends = jnp.where(mine, pltpu.roll(tail, (EDGE * k + EDGE) % 128, 1), ends)
                starts = jnp.where(mine, pltpu.roll(head, EDGE * k, 1) if k else head, starts)
            strips[0, g] = ends.astype(jnp.bfloat16)
            strips[1, g] = starts.astype(jnp.bfloat16)
            return carry

        lax.fori_loop(0, visits // GROUP, body, 0)

    def unpack_columns():
        left_ok = (col > 0).astype(jnp.float32)
        right_ok = (col < cols_n - 1).astype(jnp.float32)
        lane = lax.broadcasted_iota(jnp.int32, (256 + 2 * EDGE, 128), 1)

        def body(g, carry):
            lefts = got[0, g].astype(jnp.float32) * left_ok
            rights = got[1, g].astype(jnp.float32) * right_ok
            for k in range(GROUP):
                lo = pltpu.roll(lefts, (128 - EDGE * k) % 128, 1) if k else lefts
                hi = pltpu.roll(rights, (128 + EDGE - EDGE * k) % 128, 1) if k != 1 else rights
                tile = jnp.where(lane < EDGE, lo, jnp.where(lane < 2 * EDGE, hi, 0.0))
                win[g * GROUP + k, :, 256:384] = tile.astype(jnp.bfloat16)
            return carry

        lax.fori_loop(0, visits // GROUP, body, 0)

    def position(index, axis, size):
        pixel = (index * 256 + lax.broadcasted_iota(jnp.int32, (256, 256), axis)).astype(jnp.float32)
        return (pixel + 0.5) * (2.0 / (256 * size)) - 1.0

    def build_tables():
        def rows_of(b, carry):
            shape = (128, 128 + 2 * EDGE)
            tap = lax.broadcasted_iota(jnp.int32, shape, 1) - lax.broadcasted_iota(jnp.int32, shape, 0)
            table = jnp.zeros(shape, jnp.float32)
            for k in range(taps):
                table = jnp.where(tap == k + EDGE - half, rtaps_ref[b, k], table)
            row_table[pl.ds(pl.multiple_of(b * 128, 128), 128)] = table.astype(jnp.bfloat16)
            return carry

        lax.fori_loop(0, bases, rows_of, 0)

        def cols_of(b, carry):
            for part in range(3):
                shape = (128, 256)
                line = lax.broadcasted_iota(jnp.int32, shape, 0)
                source = line + 128 * part
                if part == 2:
                    source = jnp.where(
                        line < EDGE, line - EDGE, jnp.where(line < 2 * EDGE, line + 256 - EDGE, -1000)
                    )
                tap = source - lax.broadcasted_iota(jnp.int32, shape, 1)
                table = jnp.zeros(shape, jnp.float32)
                for k in range(taps):
                    table = jnp.where(tap == k - half, ctaps_ref[b, k], table)
                col_table[b, 128 * part : 128 * part + 128] = table.astype(jnp.bfloat16)
            return carry

        lax.fori_loop(0, bases, cols_of, 0)

    def correlate(start, stop):
        def body(v, carry):
            rows_pos = position(row, 0, rows_n)
            cols_pos = position(col, 1, cols_n)
            for h in range(2):
                first = jnp.dot(
                    row_table[...], win[v, 128 * h : 128 * h + 128 + 2 * EDGE],
                    preferred_element_type=jnp.float32,
                )
                for b in range(bases):
                    first_ref[b, 128 * h : 128 * h + 128] = first[128 * b : 128 * b + 128].astype(
                        jnp.bfloat16
                    )
            acc = jnp.zeros((256, 256), jnp.float32)
            for b in range(bases):
                second = jnp.dot(first_ref[b], col_table[b], preferred_element_type=jnp.float32)
                weight = coef_ref[v, b * 3] + coef_ref[v, b * 3 + 1] * rows_pos
                acc += (weight + coef_ref[v, b * 3 + 2] * cols_pos) * second
            matched[v] = acc
            return carry

        lax.fori_loop(start, stop, body, 0)

    def combine():
        for sr in range(2):
            for sc in range(2):
                rows, cols = slice(128 * sr, 128 * sr + 128), slice(128 * sc, 128 * sc + 128)

                def body(v, carry, rows=rows, cols=cols, quarter=sr * 2 + sc):
                    numer, total = carry
                    weight = summed(v * 4 + quarter).astype(jnp.float32)
                    return numer + weight * matched[v, rows, cols], total + weight

                zero = jnp.zeros((128, 128), jnp.float32)
                numer, total = lax.fori_loop(0, visits, body, (zero, zero + 1.0))
                numer_out[rows, cols] = numer / total
                total_out[rows, cols] = total

    stage1(0)
    build_tables()
    stage2(0)
    stage1(1)
    stage3(0)
    stage2(1)
    stage3(1, (0,))
    stage4(0)
    segments(0)
    place_flux()
    down.start()
    up.start()
    down.wait()
    up.wait()
    pack_columns()
    to_right.start()
    to_left.start()
    stage3(1, (1,))
    to_right.wait()
    to_left.wait()
    unpack_columns()
    stage3(1, (3,))
    correlate(0, 2)
    stage3(1, (2,))
    correlate(2, visits)
    stage4(1)
    segments(1)
    combine()
    drain(0)
    drain(1)


def route(slots, collective, order, fresh, last, has, coef, send, row_taps, col_taps):
    visits, bases = coef.shape[0], row_taps.shape[0]
    count = len(units_of(slots))
    dma = pltpu.SemaphoreType.DMA
    hop = jax.ShapeDtypeStruct((2, slots, 4, 4, 4, 128, 128), jnp.bfloat16)
    image = jax.ShapeDtypeStruct((256, 256), jnp.float32)
    smem = pl.BlockSpec(memory_space=pltpu.SMEM)
    vmem = pl.BlockSpec(memory_space=pltpu.VMEM)
    anywhere = pl.BlockSpec(memory_space=pl.ANY)
    coadd, weight, _, _ = pl.pallas_call(
        functools.partial(route_kernel, slots, visits, bases),
        out_shape=[image, image, hop, hop],
        in_specs=[smem] * 7 + [anywhere],
        out_specs=[vmem] * 2 + [anywhere] * 2,
        scratch_shapes=[
            pltpu.VMEM((2, slots, 4, 4, 4, 128, 128), jnp.bfloat16),
            pltpu.VMEM((2, slots, 4, 4, 4, 128, 128), jnp.bfloat16),
            pltpu.VMEM((256, 128, 128), jnp.bfloat16),
            pltpu.VMEM((visits, 256 + 2 * EDGE, 384), jnp.bfloat16),
            pltpu.VMEM((visits, 256, 256), jnp.float32),
            pltpu.VMEM((2, visits // GROUP, 256 + 2 * EDGE, 128), jnp.bfloat16),
            pltpu.VMEM((2, visits // GROUP, 256 + 2 * EDGE, 128), jnp.bfloat16),
            pltpu.VMEM((bases * 128, 128 + 2 * EDGE), jnp.bfloat16),
            pltpu.VMEM((bases, 384, 256), jnp.bfloat16),
            pltpu.VMEM((bases, 256, 384), jnp.bfloat16),
            dma((2, count, 4)), dma((2, count, 4)),
            dma((2, count, 4, 4)), dma((2, count, 4, 4)),
            dma((2, count, 4, 4)), dma((2, count, 4, 4)),
            dma((2, count, 4)), dma((2, count, 4)),
            dma((2, count, 4)), dma((4,)), dma((4,)),
        ],
        compiler_params=pltpu.CompilerParams(
            collective_id=collective, has_side_effects=True, vmem_limit_bytes=63 * 2**20
        ),
    )(order, fresh, last, has, coef, row_taps, col_taps, send)
    return coadd, weight


def local(flux_blocks, ivar_blocks, dest_cell, visit_id, slot_id, row_taps, col_taps, kernel_coef):
    slots = 4
    blocks = flux_blocks.shape[0]
    visits, bases = kernel_coef.shape[:2]
    bins = visits * 4
    me_row, me_col = lax.axis_index("celly"), lax.axis_index("cellx")
    my_chip, my_core = me_row * 4 + me_col // 2, me_col % 2

    target = dest_cell[:, 0]
    chip = target // 2
    i = jnp.arange(blocks)
    rank = jnp.sum((chip[:, None] == chip[None, :]) & (i[None, :] < i[:, None]), axis=1)
    spot = rank * CHIPS + chip
    hit = spot[None, :] == jnp.arange(slots * CHIPS)[:, None]
    index = jnp.sum(jnp.where(hit, i[None, :], 0), axis=1).astype(jnp.int32)
    code = (target % 2) * bins + visit_id * 4 + slot_id
    tags = jnp.sum(jnp.where(hit, code[None, :] + 1, 0), axis=1) - 1
    tags = jnp.zeros((8, 128), jnp.int32).at[: slots * CHIPS // 128].set(
        tags.astype(jnp.int32).reshape(-1, 128)
    )
    per = 32
    send, tags = pl.pallas_call(
        gather_kernel,
        out_shape=[
            jax.ShapeDtypeStruct((2, slots, CHIPS, 128, 128), jnp.bfloat16),
            jax.ShapeDtypeStruct((4, 4, 4, 2, 8, 128), jnp.int32),
        ],
        grid_spec=pltpu.PrefetchScalarGridSpec(
            num_scalar_prefetch=1,
            grid=(2, slots * CHIPS // per),
            in_specs=[pl.BlockSpec((blocks, 128, 128), lambda a, s, ix: (0, 0, 0))] * 2
            + [pl.BlockSpec(memory_space=pltpu.VMEM)],
            out_specs=[
                pl.BlockSpec(
                    (None, None, per, 128, 128),
                    lambda a, s, ix: (a, s // (CHIPS // per), s % (CHIPS // per), 0, 0),
                ),
                pl.BlockSpec(memory_space=pl.ANY),
            ],
            scratch_shapes=[
                pltpu.SemaphoreType.DMA((4, 4)),
                pltpu.SemaphoreType.DMA((4, 4)),
                pltpu.SemaphoreType.DMA,
            ],
        ),
        compiler_params=pltpu.CompilerParams(
            collective_id=2, has_side_effects=True, vmem_limit_bytes=40 * 2**20
        ),
    )(index, flux_blocks, ivar_blocks, tags)
    send = send.reshape(2, slots, 4, 4, 4, 128, 128)
    tags = tags[:, :, :, :, : slots * CHIPS // 128].reshape(2 * CHIPS, slots * CHIPS)

    mine = lax.dynamic_index_in_dim(
        tags.reshape(CHIPS, 2, slots, CHIPS), my_chip, axis=3, keepdims=False
    )
    lanes = jnp.where(my_core == 0, mine, mine[:, ::-1])
    overflow = jnp.any(tags[:, 3 * CHIPS :] >= 0)

    row_taps_f, col_taps_f = row_taps.astype(jnp.float32), col_taps.astype(jnp.float32)
    coef = kernel_coef.reshape(visits, bases * 3)

    def run(number, collective):
        keys = jnp.transpose(lanes[:, :, :number], (1, 2, 0)).reshape(-1) - my_core * bins
        total = keys.shape[0]
        keys = jnp.where((keys >= 0) & (keys < bins), keys, bins)
        order_key = keys * total + jnp.arange(total)
        rank_of = jnp.sum((order_key[None, :] < order_key[:, None]).astype(jnp.int32), axis=1)
        spots = jnp.arange(256)
        order = jnp.sum(
            jnp.where(rank_of[None, :] == spots[:, None], jnp.arange(total)[None, :], 0), axis=1
        ).astype(jnp.int32)
        bin_ids = jnp.arange(bins)
        upto = jnp.sum((keys[None, :] <= bin_ids[:, None]).astype(jnp.int32), axis=1)
        below = jnp.sum((keys[None, :] < bin_ids[:, None]).astype(jnp.int32), axis=1)
        has = (upto > below).astype(jnp.int32)
        fresh = jnp.any(
            (below[None, :] == spots[:, None]) & (has[None, :] > 0), axis=1
        ).astype(jnp.int32)
        last = jnp.maximum(upto - 1, 0).astype(jnp.int32)
        return route(
            number, collective, order, fresh, last, has, coef, send, row_taps_f, col_taps_f,
        )

    return lax.cond(overflow, lambda: run(4, 1), lambda: run(3, 0))


def solution(mesh):
    placed = (
        P(("celly", "cellx"), None, None),
        P(("celly", "cellx"), None, None),
        P(("celly", "cellx"), None),
        P(("celly", "cellx")),
        P(("celly", "cellx")),
        P(),
        P(),
        P(),
    )
    return jax.shard_map(
        local,
        mesh=mesh,
        in_specs=placed,
        out_specs=(P("celly", "cellx"), P("celly", "cellx")),
        check_vma=False,
    )
```

```python
import functools

import jax
import jax.numpy as jnp
from jax import lax
from jax.experimental import pallas as pl
from jax.experimental.pallas import tpu as pltpu
from jax.sharding import PartitionSpec as P

MESH = pl.DeviceIdType.MESH
SIDE = 4
CHIPS = SIDE**3
EDGE = 32
STEP = 4
GROUP = 4


def coordinates():
    row, col = lax.axis_index("celly"), lax.axis_index("cellx")
    return [row // SIDE, row % SIDE, col // 2, col % 2]


def device(q):
    return (q[0] * SIDE + q[1], q[2] * 2 + q[3])


def shifted(q, axis, d, n=SIDE):
    r = list(q)
    r[axis] = lax.rem(q[axis] + d, n)
    return r


def gather_kernel(
    index_ref, flux_ref, ivar_ref, tag_ref, flux_out, ivar_out, all_ref, send, recv, own
):
    step = pl.program_id(0)
    per = flux_out.shape[0]
    x, y, z, core = q = coordinates()
    partner = shifted(q, 3, 1, 2)
    whole = slice(None)
    hops = [
        [(0, partner, (x, y, z, core))],
        [(d, shifted(q, 0, d), (x, y, z)) for d in (1, 2, 3)],
        [(d, shifted(q, 1, d), (whole, y, z)) for d in (1, 2, 3)],
        [(d, shifted(q, 2, d), (whole, whole, z)) for d in (1, 2, 3)],
    ]
    arrivals = [
        [(0, (x, y, z, 1 - core))],
        [(d, (lax.rem(x + SIDE - d, SIDE), y, z)) for d in (1, 2, 3)],
        [(d, (whole, lax.rem(y + SIDE - d, SIDE), z)) for d in (1, 2, 3)],
        [(d, (whole, whole, lax.rem(z + SIDE - d, SIDE))) for d in (1, 2, 3)],
    ]

    def copies(hop):
        return [
            pltpu.make_async_remote_copy(
                tag_ref if hop == 0 else all_ref.at[where], all_ref.at[where],
                send.at[hop, d], recv.at[hop, d], device_id=device(to), device_id_type=MESH,
            )
            for d, to, where in hops[hop]
        ]

    def begin():
        barrier = pltpu.get_barrier_semaphore()
        peers = [device(shifted(q, a, d)) for a in range(3) for d in (1, 2, 3)] + [device(partner)]
        for peer in peers:
            pl.semaphore_signal(barrier, inc=1, device_id=peer, device_id_type=MESH)
        mine = pltpu.make_async_copy(tag_ref, all_ref.at[x, y, z, core], own)
        mine.start()
        pl.semaphore_wait(barrier, len(peers))
        for copy in copies(0):
            copy.start()
        mine.wait()

    def advance(hop):
        for d, where in arrivals[hop]:
            place = all_ref.at[where]
            pltpu.make_async_remote_copy(
                place, place, send.at[hop, d], recv.at[hop, d],
                device_id=device(partner), device_id_type=MESH,
            ).wait_recv()
        if hop < 3:
            for copy in copies(hop + 1):
                copy.start()
        else:
            for earlier in range(4):
                for copy in copies(earlier):
                    copy.wait_send()

    pl.when(step == 0)(begin)

    def body(i, carry):
        for k in range(STEP):
            block = index_ref[step * per + STEP * i + k]
            flux_out[STEP * i + k] = flux_ref[block]
            ivar_out[STEP * i + k] = ivar_ref[block]
        return carry

    lax.fori_loop(0, per // STEP, body, 0)
    for hop, moment in enumerate((4, 8, 12, 15)):
        pl.when(step == moment)(functools.partial(advance, hop))


def units_of(slots):
    units = [(s, 0, 128, s) for s in range(3)]
    if slots == 4:
        units += [(3, 0, 48, 0), (3, 48, 48, 1), (3, 96, 32, 2)]
    return units


def route_kernel(
    slots, visits, bases,
    order_ref, fresh_ref, last_ref, has_ref, coef_ref, rtaps_ref, ctaps_ref, t0_flux, t0_ivar,
    numer_out, total_out, t1, t2,
    t_flux, t_ivar, seg, win, matched, strips, got, row_table, col_table, first_ref,
    s1, r1, s2, r2, s3, r3, s4, r4, ls, hs, hr,
):
    t, t0 = (t_flux, t_ivar), (t0_flux, t0_ivar)
    q = coordinates()
    row, col = lax.axis_index("celly"), lax.axis_index("cellx")
    rows_n, cols_n = lax.axis_size("celly"), lax.axis_size("cellx")
    taps = rtaps_ref.shape[1]
    half = (taps - 1) // 2
    units = units_of(slots)
    count = len(units)
    partner = shifted(q, 3, 1, 2)
    above = (lax.rem(row + rows_n - 1, rows_n), col)
    below = (lax.rem(row + 1, rows_n), col)
    left = (row, lax.rem(col + cols_n - 1, cols_n))
    right = (row, lax.rem(col + 1, cols_n))

    barrier = pltpu.get_barrier_semaphore()
    peers = [device(shifted(q, a, d)) for a in range(3) for d in (1, 2, 3)]
    peers += [device(partner), above, below, left, right]
    for peer in peers:
        pl.semaphore_signal(barrier, inc=1, device_id=peer, device_id_type=MESH)
    pl.semaphore_wait(barrier, len(peers))

    def remote(src, dst, send, recv, to):
        return pltpu.make_async_remote_copy(
            src, dst, send, recv, device_id=to, device_id_type=MESH
        )

    def at(ref, unit, lead, where):
        slot, start, rows, _ = units[unit]
        index = [where.get(axis, slice(None)) for axis in range(3)]
        return ref.at[(*lead, slot, *index, pl.ds(start, rows))]

    def axes(unit):
        a = units[unit][3]
        return a, (a + 1) % 3, (a + 2) % 3

    def first_hop(arr, u, d):
        a, b, c = axes(u)
        to = shifted(q, a, d)
        return remote(
            at(t0[arr], u, (), {a: to[a]}), at(t1, u, (arr,), {a: q[a]}),
            s1.at[arr, u, d], r1.at[arr, u, q[a]], device(to),
        )

    def first_arrival(arr, u, da):
        a, b, c = axes(u)
        asrc = lax.rem(q[a] + da, SIDE)
        place = at(t1, u, (arr,), {a: asrc})
        return remote(place, place, s1.at[arr, u, da], r1.at[arr, u, asrc], device(q))

    def hopped(arr, u, da, where):
        return at(t1, u, (arr,), where) if da else at(t0[arr], u, (), where)

    def second_hop(arr, u, da, d):
        a, b, c = axes(u)
        to = shifted(q, b, d)
        asrc = lax.rem(q[a] + da, SIDE)
        return remote(
            hopped(arr, u, da, {a: asrc, b: to[b]}),
            at(t2, u, (arr,), {a: asrc, b: q[b]}),
            s2.at[arr, u, d, da], r2.at[arr, u, q[b], asrc], device(to),
        )

    def second_arrival(arr, u, db, da):
        a, b, c = axes(u)
        asrc = lax.rem(q[a] + da, SIDE)
        bsrc = lax.rem(q[b] + db, SIDE)
        place = at(t2, u, (arr,), {a: asrc, b: bsrc})
        return remote(place, place, s2.at[arr, u, db, da], r2.at[arr, u, bsrc, asrc], device(q))

    def third_sources(arr, u, db, cc):
        a, b, c = axes(u)
        bsrc = lax.rem(q[b] + db, SIDE)
        if db:
            return [(at(t2, u, (arr,), {b: bsrc, c: cc}), {b: bsrc, c: q[c]})]
        pairs = []
        for da in range(SIDE):
            asrc = lax.rem(q[a] + da, SIDE)
            source = hopped(arr, u, da, {a: asrc, b: bsrc, c: cc})
            pairs.append((source, {a: asrc, b: bsrc, c: q[c]}))
        return pairs

    def third_hop(arr, u, db, d):
        a, b, c = axes(u)
        to = shifted(q, c, d)
        bsrc = lax.rem(q[b] + db, SIDE)
        return [
            remote(source, at(t[arr], u, (0,), where), s3.at[arr, u, d, db], r3.at[arr, u, q[c], bsrc], device(to))
            for source, where in third_sources(arr, u, db, to[c])
        ]

    def third_whole(arr, u, db, d):
        a, b, c = axes(u)
        bsrc = lax.rem(q[b] + db, SIDE)
        csrc = lax.rem(q[c] + d, SIDE)
        place = at(t[arr], u, (0,), {b: bsrc, c: csrc})
        return remote(place, place, s3.at[arr, u, d, db], r3.at[arr, u, csrc, bsrc], device(q))

    def third_stay(arr, u, db):
        a, b, c = axes(u)
        return [
            pltpu.make_async_copy(source, at(t[arr], u, (0,), where), ls.at[arr, u, db])
            for source, where in third_sources(arr, u, db, q[c])
        ]

    def stay_whole(arr, u, db):
        a, b, c = axes(u)
        place = at(t[arr], u, (0,), {b: lax.rem(q[b] + db, SIDE), c: q[c]})
        return pltpu.make_async_copy(place, place, ls.at[arr, u, db])

    def fourth_hop(arr, u, dc):
        a, b, c = axes(u)
        csrc = lax.rem(q[c] + dc, SIDE)
        return remote(
            at(t[arr], u, (0,), {c: csrc}), at(t[arr], u, (1,), {c: csrc}),
            s4.at[arr, u, dc], r4.at[arr, u, csrc], device(partner),
        )

    def stage1(arr):
        for d in (2, 1, 3):
            for u in range(count):
                first_hop(arr, u, d).start()

    def stage2(arr, groups=(0, 1, 3, 2)):
        for da in groups:
            for u in range(count):
                if da:
                    first_arrival(arr, u, da).wait_recv()
                for d in (2, 1, 3):
                    second_hop(arr, u, da, d).start()

    def stage3(arr, groups=(0, 1, 3, 2)):
        for db in groups:
            for u in range(count):
                if db:
                    for da in range(SIDE):
                        second_arrival(arr, u, db, da).wait_recv()
                for d in (2, 1, 3):
                    for copy in third_hop(arr, u, db, d):
                        copy.start()
                for copy in third_stay(arr, u, db):
                    copy.start()

    def stage4(arr):
        for dc in (0, 1, 3, 2):
            for u in range(count):
                for db in range(SIDE):
                    if dc:
                        third_whole(arr, u, db, dc).wait_recv()
                    else:
                        stay_whole(arr, u, db).wait()
                fourth_hop(arr, u, dc).start()
        for dc in (0, 1, 3, 2):
            for u in range(count):
                fourth_hop(arr, u, dc).wait()

    def drain(arr):
        for u in range(count):
            for d in (1, 2, 3):
                first_hop(arr, u, d).wait_send()
                for e in range(SIDE):
                    second_hop(arr, u, e, d).wait_send()
                    third_whole(arr, u, e, d).wait_send()

    def segments(arr):
        def body(step, total):
            for k in range(STEP):
                p = step * STEP + k
                i = order_ref[p]
                block = t[arr][i // (CHIPS * slots), (i // CHIPS) % slots,
                          (i // 16) % 4, (i // 4) % 4, i % 4].astype(jnp.float32)
                total = jnp.where(fresh_ref[p] > 0, block, total + block)
                seg[p] = total.astype(jnp.bfloat16)
            return total

        lax.fori_loop(0, seg.shape[0] // STEP, body, jnp.zeros((128, 128), jnp.float32))

    def summed(key):
        block = seg[last_ref[key]]
        return jnp.where(has_ref[key] > 0, block, jnp.zeros_like(block))

    def place_flux():
        def body(v, carry):
            for sr in range(2):
                for sc in range(2):
                    win[v, EDGE + 128 * sr : EDGE + 128 * sr + 128, 128 * sc : 128 * sc + 128] = summed(
                        v * 4 + sr * 2 + sc
                    )
            return carry

        lax.fori_loop(0, visits, body, 0)

    down = remote(
        win.at[:, pl.ds(256, EDGE), pl.ds(0, 256)],
        win.at[:, pl.ds(0, EDGE), pl.ds(0, 256)],
        hs.at[0], hr.at[0], below,
    )
    up = remote(
        win.at[:, pl.ds(EDGE, EDGE), pl.ds(0, 256)],
        win.at[:, pl.ds(256 + EDGE, EDGE), pl.ds(0, 256)],
        hs.at[1], hr.at[1], above,
    )
    to_right = remote(strips.at[0], got.at[0], hs.at[2], hr.at[2], right)
    to_left = remote(strips.at[1], got.at[1], hs.at[3], hr.at[3], left)

    def pack_columns():
        top_ok = (row > 0).astype(jnp.float32)
        bottom_ok = (row < rows_n - 1).astype(jnp.float32)

        def clear(v, carry):
            lo = win[v, 0:EDGE, 0:256].astype(jnp.float32) * top_ok
            hi = win[v, 256 + EDGE : 256 + 2 * EDGE, 0:256].astype(jnp.float32) * bottom_ok
            win[v, 0:EDGE, 0:256] = lo.astype(jnp.bfloat16)
            win[v, 256 + EDGE : 256 + 2 * EDGE, 0:256] = hi.astype(jnp.bfloat16)
            return carry

        lax.fori_loop(0, visits, clear, 0)
        lane = lax.broadcasted_iota(jnp.int32, (256 + 2 * EDGE, 128), 1)

        def body(g, carry):
            ends = jnp.zeros(lane.shape, jnp.float32)
            starts = jnp.zeros(lane.shape, jnp.float32)
            for k in range(GROUP):
                mine = (lane >= EDGE * k) & (lane < EDGE * k + EDGE)
                tail = win[g * GROUP + k, :, 128:256].astype(jnp.float32)
                head = win[g * GROUP + k, :, 0:128].astype(jnp.float32)
                ends = jnp.where(mine, pltpu.roll(tail, (EDGE * k + EDGE) % 128, 1), ends)
                starts = jnp.where(mine, pltpu.roll(head, EDGE * k, 1) if k else head, starts)
            strips[0, g] = ends.astype(jnp.bfloat16)
            strips[1, g] = starts.astype(jnp.bfloat16)
            return carry

        lax.fori_loop(0, visits // GROUP, body, 0)

    def unpack_columns():
        left_ok = (col > 0).astype(jnp.float32)
        right_ok = (col < cols_n - 1).astype(jnp.float32)
        lane = lax.broadcasted_iota(jnp.int32, (256 + 2 * EDGE, 128), 1)

        def body(g, carry):
            lefts = got[0, g].astype(jnp.float32) * left_ok
            rights = got[1, g].astype(jnp.float32) * right_ok
            for k in range(GROUP):
                lo = pltpu.roll(lefts, (128 - EDGE * k) % 128, 1) if k else lefts
                hi = pltpu.roll(rights, (128 + EDGE - EDGE * k) % 128, 1) if k != 1 else rights
                tile = jnp.where(lane < EDGE, lo, jnp.where(lane < 2 * EDGE, hi, 0.0))
                win[g * GROUP + k, :, 256:384] = tile.astype(jnp.bfloat16)
            return carry

        lax.fori_loop(0, visits // GROUP, body, 0)

    def position(index, axis, size):
        pixel = (index * 256 + lax.broadcasted_iota(jnp.int32, (256, 256), axis)).astype(jnp.float32)
        return (pixel + 0.5) * (2.0 / (256 * size)) - 1.0

    def build_tables():
        def rows_of(b, carry):
            shape = (128, 128 + 2 * EDGE)
            tap = lax.broadcasted_iota(jnp.int32, shape, 1) - lax.broadcasted_iota(jnp.int32, shape, 0)
            table = jnp.zeros(shape, jnp.float32)
            for k in range(taps):
                table = jnp.where(tap == k + EDGE - half, rtaps_ref[b, k], table)
            row_table[pl.ds(pl.multiple_of(b * 128, 128), 128)] = table.astype(jnp.bfloat16)
            return carry

        lax.fori_loop(0, bases, rows_of, 0)

        def cols_of(b, carry):
            for part in range(3):
                shape = (128, 256)
                line = lax.broadcasted_iota(jnp.int32, shape, 0)
                source = line + 128 * part
                if part == 2:
                    source = jnp.where(
                        line < EDGE, line - EDGE, jnp.where(line < 2 * EDGE, line + 256 - EDGE, -1000)
                    )
                tap = source - lax.broadcasted_iota(jnp.int32, shape, 1)
                table = jnp.zeros(shape, jnp.float32)
                for k in range(taps):
                    table = jnp.where(tap == k - half, ctaps_ref[b, k], table)
                col_table[b, 128 * part : 128 * part + 128] = table.astype(jnp.bfloat16)
            return carry

        lax.fori_loop(0, bases, cols_of, 0)

    def correlate(start, stop):
        def body(v, carry):
            rows_pos = position(row, 0, rows_n)
            cols_pos = position(col, 1, cols_n)
            for h in range(2):
                first = jnp.dot(
                    row_table[...], win[v, 128 * h : 128 * h + 128 + 2 * EDGE],
                    preferred_element_type=jnp.float32,
                )
                for b in range(bases):
                    first_ref[b, 128 * h : 128 * h + 128] = first[128 * b : 128 * b + 128].astype(
                        jnp.bfloat16
                    )
            acc = jnp.zeros((256, 256), jnp.float32)
            for b in range(bases):
                second = jnp.dot(first_ref[b], col_table[b], preferred_element_type=jnp.float32)
                weight = coef_ref[v, b * 3] + coef_ref[v, b * 3 + 1] * rows_pos
                acc += (weight + coef_ref[v, b * 3 + 2] * cols_pos) * second
            matched[v] = acc
            return carry

        lax.fori_loop(start, stop, body, 0)

    def combine():
        for sr in range(2):
            for sc in range(2):
                rows, cols = slice(128 * sr, 128 * sr + 128), slice(128 * sc, 128 * sc + 128)

                def body(v, carry, rows=rows, cols=cols, quarter=sr * 2 + sc):
                    numer, total = carry
                    weight = summed(v * 4 + quarter).astype(jnp.float32)
                    return numer + weight * matched[v, rows, cols], total + weight

                zero = jnp.zeros((128, 128), jnp.float32)
                numer, total = lax.fori_loop(0, visits, body, (zero, zero + 1.0))
                numer_out[rows, cols] = numer / total
                total_out[rows, cols] = total

    stage1(0)
    build_tables()
    stage2(0)
    stage3(0)
    stage1(1)
    stage2(1, (0,))
    stage4(0)
    segments(0)
    place_flux()
    down.start()
    up.start()
    down.wait()
    up.wait()
    pack_columns()
    to_right.start()
    to_left.start()
    stage2(1, (1, 3, 2))
    stage3(1, (0,))
    to_right.wait()
    to_left.wait()
    unpack_columns()
    correlate(0, visits // 2)
    stage3(1, (1, 3, 2))
    correlate(visits // 2, visits)
    stage4(1)
    segments(1)
    combine()
    drain(0)
    drain(1)


def route(slots, collective, order, fresh, last, has, coef, send, row_taps, col_taps):
    visits, bases = coef.shape[0], row_taps.shape[0]
    count = len(units_of(slots))
    dma = pltpu.SemaphoreType.DMA
    hop = jax.ShapeDtypeStruct((2, slots, 4, 4, 4, 128, 128), jnp.bfloat16)
    image = jax.ShapeDtypeStruct((256, 256), jnp.float32)
    smem = pl.BlockSpec(memory_space=pltpu.SMEM)
    vmem = pl.BlockSpec(memory_space=pltpu.VMEM)
    anywhere = pl.BlockSpec(memory_space=pl.ANY)
    coadd, weight, _, _ = pl.pallas_call(
        functools.partial(route_kernel, slots, visits, bases),
        out_shape=[image, image, hop, hop],
        in_specs=[smem] * 7 + [anywhere] * 2,
        out_specs=[vmem] * 2 + [anywhere] * 2,
        scratch_shapes=[
            pltpu.VMEM((2, slots, 4, 4, 4, 128, 128), jnp.bfloat16),
            pltpu.VMEM((2, slots, 4, 4, 4, 128, 128), jnp.bfloat16),
            pltpu.VMEM((256, 128, 128), jnp.bfloat16),
            pltpu.VMEM((visits, 256 + 2 * EDGE, 384), jnp.bfloat16),
            pltpu.VMEM((visits, 256, 256), jnp.float32),
            pltpu.VMEM((2, visits // GROUP, 256 + 2 * EDGE, 128), jnp.bfloat16),
            pltpu.VMEM((2, visits // GROUP, 256 + 2 * EDGE, 128), jnp.bfloat16),
            pltpu.VMEM((bases * 128, 128 + 2 * EDGE), jnp.bfloat16),
            pltpu.VMEM((bases, 384, 256), jnp.bfloat16),
            pltpu.VMEM((bases, 256, 384), jnp.bfloat16),
            dma((2, count, 4)), dma((2, count, 4)),
            dma((2, count, 4, 4)), dma((2, count, 4, 4)),
            dma((2, count, 4, 4)), dma((2, count, 4, 4)),
            dma((2, count, 4)), dma((2, count, 4)),
            dma((2, count, 4)), dma((4,)), dma((4,)),
        ],
        compiler_params=pltpu.CompilerParams(
            collective_id=collective, has_side_effects=True, vmem_limit_bytes=63 * 2**20
        ),
    )(order, fresh, last, has, coef, row_taps, col_taps, *send)
    return coadd, weight


def local(flux_blocks, ivar_blocks, dest_cell, visit_id, slot_id, row_taps, col_taps, kernel_coef):
    slots = 4
    blocks = flux_blocks.shape[0]
    visits, bases = kernel_coef.shape[:2]
    bins = visits * 4
    me_row, me_col = lax.axis_index("celly"), lax.axis_index("cellx")
    my_chip, my_core = me_row * 4 + me_col // 2, me_col % 2

    target = dest_cell[:, 0]
    chip = target // 2
    i = jnp.arange(blocks)
    rank = jnp.sum((chip[:, None] == chip[None, :]) & (i[None, :] < i[:, None]), axis=1)
    spot = rank * CHIPS + chip
    hit = spot[None, :] == jnp.arange(slots * CHIPS)[:, None]
    index = jnp.sum(jnp.where(hit, i[None, :], 0), axis=1).astype(jnp.int32)
    code = (target % 2) * bins + visit_id * 4 + slot_id
    tags = jnp.sum(jnp.where(hit, code[None, :] + 1, 0), axis=1) - 1
    tags = jnp.zeros((8, 128), jnp.int32).at[: slots * CHIPS // 128].set(
        tags.astype(jnp.int32).reshape(-1, 128)
    )
    per = slots * CHIPS // 16
    slot_spec = pl.BlockSpec(
        (None, per, 128, 128), lambda s, ix: (s // (CHIPS // per), s % (CHIPS // per), 0, 0)
    )
    slot_shape = jax.ShapeDtypeStruct((slots, CHIPS, 128, 128), jnp.bfloat16)
    send_flux, send_ivar, tags = pl.pallas_call(
        gather_kernel,
        out_shape=[slot_shape, slot_shape, jax.ShapeDtypeStruct((4, 4, 4, 2, 8, 128), jnp.int32)],
        grid_spec=pltpu.PrefetchScalarGridSpec(
            num_scalar_prefetch=1,
            grid=(16,),
            in_specs=[pl.BlockSpec((blocks, 128, 128), lambda s, ix: (0, 0, 0))] * 2
            + [pl.BlockSpec(memory_space=pltpu.VMEM)],
            out_specs=[slot_spec, slot_spec, pl.BlockSpec(memory_space=pl.ANY)],
            scratch_shapes=[
                pltpu.SemaphoreType.DMA((4, 4)),
                pltpu.SemaphoreType.DMA((4, 4)),
                pltpu.SemaphoreType.DMA,
            ],
        ),
        compiler_params=pltpu.CompilerParams(
            collective_id=2, has_side_effects=True, vmem_limit_bytes=40 * 2**20
        ),
    )(index, flux_blocks, ivar_blocks, tags)
    send = [part.reshape(slots, 4, 4, 4, 128, 128) for part in (send_flux, send_ivar)]
    tags = tags[:, :, :, :, : slots * CHIPS // 128].reshape(2 * CHIPS, slots * CHIPS)

    mine = lax.dynamic_index_in_dim(
        tags.reshape(CHIPS, 2, slots, CHIPS), my_chip, axis=3, keepdims=False
    )
    lanes = jnp.where(my_core == 0, mine, mine[:, ::-1])
    overflow = jnp.any(tags[:, 3 * CHIPS :] >= 0)

    row_taps_f, col_taps_f = row_taps.astype(jnp.float32), col_taps.astype(jnp.float32)
    coef = kernel_coef.reshape(visits, bases * 3)

    def run(number, collective):
        keys = jnp.transpose(lanes[:, :, :number], (1, 2, 0)).reshape(-1) - my_core * bins
        total = keys.shape[0]
        keys = jnp.where((keys >= 0) & (keys < bins), keys, bins)
        order_key = keys * total + jnp.arange(total)
        rank_of = jnp.sum((order_key[None, :] < order_key[:, None]).astype(jnp.int32), axis=1)
        spots = jnp.arange(256)
        order = jnp.sum(
            jnp.where(rank_of[None, :] == spots[:, None], jnp.arange(total)[None, :], 0), axis=1
        ).astype(jnp.int32)
        bin_ids = jnp.arange(bins)
        upto = jnp.sum((keys[None, :] <= bin_ids[:, None]).astype(jnp.int32), axis=1)
        below = jnp.sum((keys[None, :] < bin_ids[:, None]).astype(jnp.int32), axis=1)
        has = (upto > below).astype(jnp.int32)
        fresh = jnp.any(
            (below[None, :] == spots[:, None]) & (has[None, :] > 0), axis=1
        ).astype(jnp.int32)
        last = jnp.maximum(upto - 1, 0).astype(jnp.int32)
        return route(
            number, collective, order, fresh, last, has, coef, send, row_taps_f, col_taps_f,
        )

    return lax.cond(overflow, lambda: run(4, 1), lambda: run(3, 0))


def solution(mesh):
    placed = (
        P(("celly", "cellx"), None, None),
        P(("celly", "cellx"), None, None),
        P(("celly", "cellx"), None),
        P(("celly", "cellx")),
        P(("celly", "cellx")),
        P(),
        P(),
        P(),
    )
    return jax.shard_map(
        local,
        mesh=mesh,
        in_specs=placed,
        out_specs=(P("celly", "cellx"), P("celly", "cellx")),
        check_vma=False,
    )
```

```python
import functools

import jax
import jax.numpy as jnp
from jax import lax
from jax.experimental import pallas as pl
from jax.experimental.pallas import tpu as pltpu
from jax.sharding import PartitionSpec as P

MESH = pl.DeviceIdType.MESH
SIDE = 4
CHIPS = SIDE**3
EDGE = 32
STEP = 4
GROUP = 4


def coordinates():
    row, col = lax.axis_index("celly"), lax.axis_index("cellx")
    return [row // SIDE, row % SIDE, col // 2, col % 2]


def device(q):
    return (q[0] * SIDE + q[1], q[2] * 2 + q[3])


def shifted(q, axis, d, n=SIDE):
    r = list(q)
    r[axis] = lax.rem(q[axis] + d, n)
    return r


def gather_kernel(
    index_ref, flux_ref, ivar_ref, tag_ref, flux_out, ivar_out, all_ref, send, recv, own
):
    step = pl.program_id(0)
    per = flux_out.shape[0]
    x, y, z, core = q = coordinates()
    partner = shifted(q, 3, 1, 2)
    whole = slice(None)
    hops = [
        [(0, partner, (x, y, z, core))],
        [(d, shifted(q, 0, d), (x, y, z)) for d in (1, 2, 3)],
        [(d, shifted(q, 1, d), (whole, y, z)) for d in (1, 2, 3)],
        [(d, shifted(q, 2, d), (whole, whole, z)) for d in (1, 2, 3)],
    ]
    arrivals = [
        [(0, (x, y, z, 1 - core))],
        [(d, (lax.rem(x + SIDE - d, SIDE), y, z)) for d in (1, 2, 3)],
        [(d, (whole, lax.rem(y + SIDE - d, SIDE), z)) for d in (1, 2, 3)],
        [(d, (whole, whole, lax.rem(z + SIDE - d, SIDE))) for d in (1, 2, 3)],
    ]

    def copies(hop):
        return [
            pltpu.make_async_remote_copy(
                tag_ref if hop == 0 else all_ref.at[where], all_ref.at[where],
                send.at[hop, d], recv.at[hop, d], device_id=device(to), device_id_type=MESH,
            )
            for d, to, where in hops[hop]
        ]

    def begin():
        barrier = pltpu.get_barrier_semaphore()
        peers = [device(shifted(q, a, d)) for a in range(3) for d in (1, 2, 3)] + [device(partner)]
        for peer in peers:
            pl.semaphore_signal(barrier, inc=1, device_id=peer, device_id_type=MESH)
        mine = pltpu.make_async_copy(tag_ref, all_ref.at[x, y, z, core], own)
        mine.start()
        pl.semaphore_wait(barrier, len(peers))
        for copy in copies(0):
            copy.start()
        mine.wait()

    def advance(hop):
        for d, where in arrivals[hop]:
            place = all_ref.at[where]
            pltpu.make_async_remote_copy(
                place, place, send.at[hop, d], recv.at[hop, d],
                device_id=device(partner), device_id_type=MESH,
            ).wait_recv()
        if hop < 3:
            for copy in copies(hop + 1):
                copy.start()
        else:
            for earlier in range(4):
                for copy in copies(earlier):
                    copy.wait_send()

    pl.when(step == 0)(begin)

    def body(i, carry):
        for k in range(STEP):
            block = index_ref[step * per + STEP * i + k]
            flux_out[STEP * i + k] = flux_ref[block]
            ivar_out[STEP * i + k] = ivar_ref[block]
        return carry

    lax.fori_loop(0, per // STEP, body, 0)
    for hop, moment in enumerate((4, 8, 12, 15)):
        pl.when(step == moment)(functools.partial(advance, hop))


def units_of(slots):
    units = [(s, 0, 128, s) for s in range(3)]
    if slots == 4:
        units += [(3, 0, 48, 0), (3, 48, 48, 1), (3, 96, 32, 2)]
    return units


def route_kernel(
    slots, visits, bases,
    order_ref, fresh_ref, last_ref, has_ref, coef_ref, rtaps_ref, ctaps_ref, t0_flux, t0_ivar,
    numer_out, total_out, t1, t2,
    t_flux, t_ivar, seg, win, matched, strips, got, row_table, col_table, first_ref,
    s1, r1, s2, r2, s3, r3, s4, r4, ls, hs, hr,
):
    t, t0 = (t_flux, t_ivar), (t0_flux, t0_ivar)
    q = coordinates()
    row, col = lax.axis_index("celly"), lax.axis_index("cellx")
    rows_n, cols_n = lax.axis_size("celly"), lax.axis_size("cellx")
    taps = rtaps_ref.shape[1]
    half = (taps - 1) // 2
    units = units_of(slots)
    count = len(units)
    partner = shifted(q, 3, 1, 2)
    above = (lax.rem(row + rows_n - 1, rows_n), col)
    below = (lax.rem(row + 1, rows_n), col)
    left = (row, lax.rem(col + cols_n - 1, cols_n))
    right = (row, lax.rem(col + 1, cols_n))

    barrier = pltpu.get_barrier_semaphore()
    peers = [device(shifted(q, a, d)) for a in range(3) for d in (1, 2, 3)]
    peers += [device(partner), above, below, left, right]
    for peer in peers:
        pl.semaphore_signal(barrier, inc=1, device_id=peer, device_id_type=MESH)
    pl.semaphore_wait(barrier, len(peers))

    def remote(src, dst, send, recv, to):
        return pltpu.make_async_remote_copy(
            src, dst, send, recv, device_id=to, device_id_type=MESH
        )

    def at(ref, unit, lead, where):
        slot, start, rows, _ = units[unit]
        index = [where.get(axis, slice(None)) for axis in range(3)]
        return ref.at[(*lead, slot, *index, pl.ds(start, rows))]

    def axes(unit):
        a = units[unit][3]
        return a, (a + 1) % 3, (a + 2) % 3

    def first_hop(arr, u, d):
        a, b, c = axes(u)
        to = shifted(q, a, d)
        return remote(
            at(t0[arr], u, (), {a: to[a]}), at(t1, u, (arr,), {a: q[a]}),
            s1.at[arr, u, d], r1.at[arr, u, q[a]], device(to),
        )

    def first_arrival(arr, u, da):
        a, b, c = axes(u)
        asrc = lax.rem(q[a] + da, SIDE)
        place = at(t1, u, (arr,), {a: asrc})
        return remote(place, place, s1.at[arr, u, da], r1.at[arr, u, asrc], device(q))

    def hopped(arr, u, da, where):
        return at(t1, u, (arr,), where) if da else at(t0[arr], u, (), where)

    def second_hop(arr, u, da, d):
        a, b, c = axes(u)
        to = shifted(q, b, d)
        asrc = lax.rem(q[a] + da, SIDE)
        return remote(
            hopped(arr, u, da, {a: asrc, b: to[b]}),
            at(t2, u, (arr,), {a: asrc, b: q[b]}),
            s2.at[arr, u, d, da], r2.at[arr, u, q[b], asrc], device(to),
        )

    def second_arrival(arr, u, db, da):
        a, b, c = axes(u)
        asrc = lax.rem(q[a] + da, SIDE)
        bsrc = lax.rem(q[b] + db, SIDE)
        place = at(t2, u, (arr,), {a: asrc, b: bsrc})
        return remote(place, place, s2.at[arr, u, db, da], r2.at[arr, u, bsrc, asrc], device(q))

    def third_sources(arr, u, db, cc):
        a, b, c = axes(u)
        bsrc = lax.rem(q[b] + db, SIDE)
        if db:
            return [(at(t2, u, (arr,), {b: bsrc, c: cc}), {b: bsrc, c: q[c]})]
        pairs = []
        for da in range(SIDE):
            asrc = lax.rem(q[a] + da, SIDE)
            source = hopped(arr, u, da, {a: asrc, b: bsrc, c: cc})
            pairs.append((source, {a: asrc, b: bsrc, c: q[c]}))
        return pairs

    def third_hop(arr, u, db, d):
        a, b, c = axes(u)
        to = shifted(q, c, d)
        bsrc = lax.rem(q[b] + db, SIDE)
        return [
            remote(source, at(t[arr], u, (0,), where), s3.at[arr, u, d, db], r3.at[arr, u, q[c], bsrc], device(to))
            for source, where in third_sources(arr, u, db, to[c])
        ]

    def third_whole(arr, u, db, d):
        a, b, c = axes(u)
        bsrc = lax.rem(q[b] + db, SIDE)
        csrc = lax.rem(q[c] + d, SIDE)
        place = at(t[arr], u, (0,), {b: bsrc, c: csrc})
        return remote(place, place, s3.at[arr, u, d, db], r3.at[arr, u, csrc, bsrc], device(q))

    def third_stay(arr, u, db):
        a, b, c = axes(u)
        return [
            pltpu.make_async_copy(source, at(t[arr], u, (0,), where), ls.at[arr, u, db])
            for source, where in third_sources(arr, u, db, q[c])
        ]

    def stay_whole(arr, u, db):
        a, b, c = axes(u)
        place = at(t[arr], u, (0,), {b: lax.rem(q[b] + db, SIDE), c: q[c]})
        return pltpu.make_async_copy(place, place, ls.at[arr, u, db])

    def fourth_hop(arr, u, dc):
        a, b, c = axes(u)
        csrc = lax.rem(q[c] + dc, SIDE)
        return remote(
            at(t[arr], u, (0,), {c: csrc}), at(t[arr], u, (1,), {c: csrc}),
            s4.at[arr, u, dc], r4.at[arr, u, csrc], device(partner),
        )

    def stage1(arr):
        for d in (2, 1, 3):
            for u in range(count):
                first_hop(arr, u, d).start()

    def stage2(arr, groups=(0, 1, 3, 2)):
        for da in groups:
            for u in range(count):
                if da:
                    first_arrival(arr, u, da).wait_recv()
                for d in (2, 1, 3):
                    second_hop(arr, u, da, d).start()

    def stage3(arr, groups=(0, 1, 3, 2)):
        for db in groups:
            for u in range(count):
                if db:
                    for da in range(SIDE):
                        second_arrival(arr, u, db, da).wait_recv()
                for d in (2, 1, 3):
                    for copy in third_hop(arr, u, db, d):
                        copy.start()
                for copy in third_stay(arr, u, db):
                    copy.start()

    def stage4(arr):
        for dc in (0, 1, 3, 2):
            for u in range(count):
                for db in range(SIDE):
                    if dc:
                        third_whole(arr, u, db, dc).wait_recv()
                    else:
                        stay_whole(arr, u, db).wait()
                fourth_hop(arr, u, dc).start()
        for dc in (0, 1, 3, 2):
            for u in range(count):
                fourth_hop(arr, u, dc).wait()

    def drain(arr):
        for u in range(count):
            for d in (1, 2, 3):
                first_hop(arr, u, d).wait_send()
                for e in range(SIDE):
                    second_hop(arr, u, e, d).wait_send()
                    third_whole(arr, u, e, d).wait_send()

    def segments(arr):
        def body(step, total):
            for k in range(STEP):
                p = step * STEP + k
                i = order_ref[p]
                block = t[arr][i // (CHIPS * slots), (i // CHIPS) % slots,
                          (i // 16) % 4, (i // 4) % 4, i % 4].astype(jnp.float32)
                total = jnp.where(fresh_ref[p] > 0, block, total + block)
                seg[p] = total.astype(jnp.bfloat16)
            return total

        lax.fori_loop(0, seg.shape[0] // STEP, body, jnp.zeros((128, 128), jnp.float32))

    def summed(key):
        block = seg[last_ref[key]]
        return jnp.where(has_ref[key] > 0, block, jnp.zeros_like(block))

    def place_flux():
        def body(v, carry):
            for sr in range(2):
                for sc in range(2):
                    win[v, EDGE + 128 * sr : EDGE + 128 * sr + 128, 128 * sc : 128 * sc + 128] = summed(
                        v * 4 + sr * 2 + sc
                    )
            return carry

        lax.fori_loop(0, visits, body, 0)

    down = remote(
        win.at[:, pl.ds(256, EDGE), pl.ds(0, 256)],
        win.at[:, pl.ds(0, EDGE), pl.ds(0, 256)],
        hs.at[0], hr.at[0], below,
    )
    up = remote(
        win.at[:, pl.ds(EDGE, EDGE), pl.ds(0, 256)],
        win.at[:, pl.ds(256 + EDGE, EDGE), pl.ds(0, 256)],
        hs.at[1], hr.at[1], above,
    )
    to_right = remote(strips.at[0], got.at[0], hs.at[2], hr.at[2], right)
    to_left = remote(strips.at[1], got.at[1], hs.at[3], hr.at[3], left)

    def pack_columns():
        top_ok = (row > 0).astype(jnp.float32)
        bottom_ok = (row < rows_n - 1).astype(jnp.float32)

        def clear(v, carry):
            lo = win[v, 0:EDGE, 0:256].astype(jnp.float32) * top_ok
            hi = win[v, 256 + EDGE : 256 + 2 * EDGE, 0:256].astype(jnp.float32) * bottom_ok
            win[v, 0:EDGE, 0:256] = lo.astype(jnp.bfloat16)
            win[v, 256 + EDGE : 256 + 2 * EDGE, 0:256] = hi.astype(jnp.bfloat16)
            return carry

        lax.fori_loop(0, visits, clear, 0)
        lane = lax.broadcasted_iota(jnp.int32, (256 + 2 * EDGE, 128), 1)

        def body(g, carry):
            ends = jnp.zeros(lane.shape, jnp.float32)
            starts = jnp.zeros(lane.shape, jnp.float32)
            for k in range(GROUP):
                mine = (lane >= EDGE * k) & (lane < EDGE * k + EDGE)
                tail = win[g * GROUP + k, :, 128:256].astype(jnp.float32)
                head = win[g * GROUP + k, :, 0:128].astype(jnp.float32)
                ends = jnp.where(mine, pltpu.roll(tail, (EDGE * k + EDGE) % 128, 1), ends)
                starts = jnp.where(mine, pltpu.roll(head, EDGE * k, 1) if k else head, starts)
            strips[0, g] = ends.astype(jnp.bfloat16)
            strips[1, g] = starts.astype(jnp.bfloat16)
            return carry

        lax.fori_loop(0, visits // GROUP, body, 0)

    def unpack_columns():
        left_ok = (col > 0).astype(jnp.float32)
        right_ok = (col < cols_n - 1).astype(jnp.float32)
        lane = lax.broadcasted_iota(jnp.int32, (256 + 2 * EDGE, 128), 1)

        def body(g, carry):
            lefts = got[0, g].astype(jnp.float32) * left_ok
            rights = got[1, g].astype(jnp.float32) * right_ok
            for k in range(GROUP):
                lo = pltpu.roll(lefts, (128 - EDGE * k) % 128, 1) if k else lefts
                hi = pltpu.roll(rights, (128 + EDGE - EDGE * k) % 128, 1) if k != 1 else rights
                tile = jnp.where(lane < EDGE, lo, jnp.where(lane < 2 * EDGE, hi, 0.0))
                win[g * GROUP + k, :, 256:384] = tile.astype(jnp.bfloat16)
            return carry

        lax.fori_loop(0, visits // GROUP, body, 0)

    def position(index, axis, size):
        shape = (256, 1) if axis == 0 else (1, 256)
        pixel = (index * 256 + lax.broadcasted_iota(jnp.int32, shape, axis)).astype(jnp.float32)
        return (pixel + 0.5) * (2.0 / (256 * size)) - 1.0

    def build_tables():
        def rows_of(b, carry):
            shape = (128, 128 + 2 * EDGE)
            tap = lax.broadcasted_iota(jnp.int32, shape, 1) - lax.broadcasted_iota(jnp.int32, shape, 0)
            table = jnp.zeros(shape, jnp.float32)
            for k in range(taps):
                table = jnp.where(tap == k + EDGE - half, rtaps_ref[b, k], table)
            row_table[pl.ds(pl.multiple_of(b * 128, 128), 128)] = table.astype(jnp.bfloat16)
            return carry

        lax.fori_loop(0, bases, rows_of, 0)

        def cols_of(b, carry):
            for part in range(3):
                shape = (128, 256)
                line = lax.broadcasted_iota(jnp.int32, shape, 0)
                source = line + 128 * part
                if part == 2:
                    source = jnp.where(
                        line < EDGE, line - EDGE, jnp.where(line < 2 * EDGE, line + 256 - EDGE, -1000)
                    )
                tap = source - lax.broadcasted_iota(jnp.int32, shape, 1)
                table = jnp.zeros(shape, jnp.float32)
                for k in range(taps):
                    table = jnp.where(tap == k - half, ctaps_ref[b, k], table)
                col_table[b, 128 * part : 128 * part + 128] = table.astype(jnp.bfloat16)
            return carry

        lax.fori_loop(0, bases, cols_of, 0)

    def correlate(start, stop):
        def body(v, carry):
            rows_pos = position(row, 0, rows_n)
            cols_pos = position(col, 1, cols_n)
            for h in range(2):
                first = jnp.dot(
                    row_table[...], win[v, 128 * h : 128 * h + 128 + 2 * EDGE],
                    preferred_element_type=jnp.float32,
                )
                for b in range(bases):
                    first_ref[b, 128 * h : 128 * h + 128] = first[128 * b : 128 * b + 128].astype(
                        jnp.bfloat16
                    )
            acc = jnp.zeros((256, 256), jnp.float32)
            for b in range(bases):
                second = jnp.dot(first_ref[b], col_table[b], preferred_element_type=jnp.float32)
                weight = coef_ref[v, b * 3] + coef_ref[v, b * 3 + 1] * rows_pos
                acc += (weight + coef_ref[v, b * 3 + 2] * cols_pos) * second
            matched[v] = acc
            return carry

        lax.fori_loop(start, stop, body, 0)

    def combine():
        for sr in range(2):
            for sc in range(2):
                rows, cols = slice(128 * sr, 128 * sr + 128), slice(128 * sc, 128 * sc + 128)

                def body(v, carry, rows=rows, cols=cols, quarter=sr * 2 + sc):
                    numer, total = carry
                    weight = summed(v * 4 + quarter).astype(jnp.float32)
                    return numer + weight * matched[v, rows, cols], total + weight

                zero = jnp.zeros((128, 128), jnp.float32)
                numer, total = lax.fori_loop(0, visits, body, (zero, zero + 1.0))
                numer_out[rows, cols] = numer / total
                total_out[rows, cols] = total

    stage1(0)
    build_tables()
    stage2(0)
    stage3(0)
    stage1(1)
    stage2(1, (0,))
    stage4(0)
    segments(0)
    place_flux()
    down.start()
    up.start()
    down.wait()
    up.wait()
    pack_columns()
    to_right.start()
    to_left.start()
    stage2(1, (1, 3, 2))
    stage3(1, (0,))
    to_right.wait()
    to_left.wait()
    unpack_columns()
    correlate(0, visits // 2)
    stage3(1, (1, 3, 2))
    correlate(visits // 2, visits)
    drain(0)
    stage4(1)
    segments(1)
    combine()
    drain(1)


def route(slots, collective, order, fresh, last, has, coef, send, row_taps, col_taps):
    visits, bases = coef.shape[0], row_taps.shape[0]
    count = len(units_of(slots))
    dma = pltpu.SemaphoreType.DMA
    hop = jax.ShapeDtypeStruct((2, slots, 4, 4, 4, 128, 128), jnp.bfloat16)
    image = jax.ShapeDtypeStruct((256, 256), jnp.float32)
    smem = pl.BlockSpec(memory_space=pltpu.SMEM)
    vmem = pl.BlockSpec(memory_space=pltpu.VMEM)
    anywhere = pl.BlockSpec(memory_space=pl.ANY)
    coadd, weight, _, _ = pl.pallas_call(
        functools.partial(route_kernel, slots, visits, bases),
        out_shape=[image, image, hop, hop],
        in_specs=[smem] * 7 + [anywhere] * 2,
        out_specs=[vmem] * 2 + [anywhere] * 2,
        scratch_shapes=[
            pltpu.VMEM((2, slots, 4, 4, 4, 128, 128), jnp.bfloat16),
            pltpu.VMEM((2, slots, 4, 4, 4, 128, 128), jnp.bfloat16),
            pltpu.VMEM((256, 128, 128), jnp.bfloat16),
            pltpu.VMEM((visits, 256 + 2 * EDGE, 384), jnp.bfloat16),
            pltpu.VMEM((visits, 256, 256), jnp.float32),
            pltpu.VMEM((2, visits // GROUP, 256 + 2 * EDGE, 128), jnp.bfloat16),
            pltpu.VMEM((2, visits // GROUP, 256 + 2 * EDGE, 128), jnp.bfloat16),
            pltpu.VMEM((bases * 128, 128 + 2 * EDGE), jnp.bfloat16),
            pltpu.VMEM((bases, 384, 256), jnp.bfloat16),
            pltpu.VMEM((bases, 256, 384), jnp.bfloat16),
            dma((2, count, 4)), dma((2, count, 4)),
            dma((2, count, 4, 4)), dma((2, count, 4, 4)),
            dma((2, count, 4, 4)), dma((2, count, 4, 4)),
            dma((2, count, 4)), dma((2, count, 4)),
            dma((2, count, 4)), dma((4,)), dma((4,)),
        ],
        compiler_params=pltpu.CompilerParams(
            collective_id=collective, has_side_effects=True, vmem_limit_bytes=63 * 2**20
        ),
    )(order, fresh, last, has, coef, row_taps, col_taps, *send)
    return coadd, weight


def local(flux_blocks, ivar_blocks, dest_cell, visit_id, slot_id, row_taps, col_taps, kernel_coef):
    slots = 4
    blocks = flux_blocks.shape[0]
    visits, bases = kernel_coef.shape[:2]
    bins = visits * 4
    me_row, me_col = lax.axis_index("celly"), lax.axis_index("cellx")
    my_chip, my_core = me_row * 4 + me_col // 2, me_col % 2

    target = dest_cell[:, 0]
    chip = target // 2
    i = jnp.arange(blocks)
    rank = jnp.sum((chip[:, None] == chip[None, :]) & (i[None, :] < i[:, None]), axis=1)
    spot = rank * CHIPS + chip
    hit = spot[None, :] == jnp.arange(slots * CHIPS)[:, None]
    index = jnp.sum(jnp.where(hit, i[None, :], 0), axis=1).astype(jnp.int32)
    code = (target % 2) * bins + visit_id * 4 + slot_id
    tags = jnp.sum(jnp.where(hit, code[None, :] + 1, 0), axis=1) - 1
    tags = jnp.zeros((8, 128), jnp.int32).at[: slots * CHIPS // 128].set(
        tags.astype(jnp.int32).reshape(-1, 128)
    )
    per = slots * CHIPS // 16
    slot_spec = pl.BlockSpec(
        (None, per, 128, 128), lambda s, ix: (s // (CHIPS // per), s % (CHIPS // per), 0, 0)
    )
    slot_shape = jax.ShapeDtypeStruct((slots, CHIPS, 128, 128), jnp.bfloat16)
    send_flux, send_ivar, tags = pl.pallas_call(
        gather_kernel,
        out_shape=[slot_shape, slot_shape, jax.ShapeDtypeStruct((4, 4, 4, 2, 8, 128), jnp.int32)],
        grid_spec=pltpu.PrefetchScalarGridSpec(
            num_scalar_prefetch=1,
            grid=(16,),
            in_specs=[pl.BlockSpec((blocks, 128, 128), lambda s, ix: (0, 0, 0))] * 2
            + [pl.BlockSpec(memory_space=pltpu.VMEM)],
            out_specs=[slot_spec, slot_spec, pl.BlockSpec(memory_space=pl.ANY)],
            scratch_shapes=[
                pltpu.SemaphoreType.DMA((4, 4)),
                pltpu.SemaphoreType.DMA((4, 4)),
                pltpu.SemaphoreType.DMA,
            ],
        ),
        compiler_params=pltpu.CompilerParams(
            collective_id=2, has_side_effects=True, vmem_limit_bytes=40 * 2**20
        ),
    )(index, flux_blocks, ivar_blocks, tags)
    send = [part.reshape(slots, 4, 4, 4, 128, 128) for part in (send_flux, send_ivar)]
    tags = tags[:, :, :, :, : slots * CHIPS // 128].reshape(2 * CHIPS, slots * CHIPS)

    mine = lax.dynamic_index_in_dim(
        tags.reshape(CHIPS, 2, slots, CHIPS), my_chip, axis=3, keepdims=False
    )
    lanes = jnp.where(my_core == 0, mine, mine[:, ::-1])
    overflow = jnp.any(tags[:, 3 * CHIPS :] >= 0)

    row_taps_f, col_taps_f = row_taps.astype(jnp.float32), col_taps.astype(jnp.float32)
    coef = kernel_coef.reshape(visits, bases * 3)

    def run(number, collective):
        keys = jnp.transpose(lanes[:, :, :number], (1, 2, 0)).reshape(-1) - my_core * bins
        total = keys.shape[0]
        keys = jnp.where((keys >= 0) & (keys < bins), keys, bins)
        order_key = keys * total + jnp.arange(total)
        rank_of = jnp.sum((order_key[None, :] < order_key[:, None]).astype(jnp.int32), axis=1)
        spots = jnp.arange(256)
        order = jnp.sum(
            jnp.where(rank_of[None, :] == spots[:, None], jnp.arange(total)[None, :], 0), axis=1
        ).astype(jnp.int32)
        bin_ids = jnp.arange(bins)
        upto = jnp.sum((keys[None, :] <= bin_ids[:, None]).astype(jnp.int32), axis=1)
        below = jnp.sum((keys[None, :] < bin_ids[:, None]).astype(jnp.int32), axis=1)
        has = (upto > below).astype(jnp.int32)
        fresh = jnp.any(
            (below[None, :] == spots[:, None]) & (has[None, :] > 0), axis=1
        ).astype(jnp.int32)
        last = jnp.maximum(upto - 1, 0).astype(jnp.int32)
        return route(
            number, collective, order, fresh, last, has, coef, send, row_taps_f, col_taps_f,
        )

    return lax.cond(overflow, lambda: run(4, 1), lambda: run(3, 0))


def solution(mesh):
    placed = (
        P(("celly", "cellx"), None, None),
        P(("celly", "cellx"), None, None),
        P(("celly", "cellx"), None),
        P(("celly", "cellx")),
        P(("celly", "cellx")),
        P(),
        P(),
        P(),
    )
    return jax.shard_map(
        local,
        mesh=mesh,
        in_specs=placed,
        out_specs=(P("celly", "cellx"), P("celly", "cellx")),
        check_vma=False,
    )
```
